512 devices in a mesh: dp: 8 (over z), fsdp: 16 (over y, x_lo), tensor: 4 (over x_hi, core).
Axes of the slice: x: 4 (x_hi: 2, x_lo: 2; x = x_hi * 2 + x_lo), y: 8, z: 8, core: 2. Of those that a mesh axis runs over, the one named last changes fastest.
Arguments:
- query: bfloat16 [8, 2048, 3072], P('dp', 'fsdp', 'tensor'), may hold values from -120 to 120
- key_in: bfloat16 [8, 2048, 3072], P('dp', 'fsdp', 'tensor'), may hold values from -9 to 9
- value: bfloat16 [8, 2048, 3072], P('dp', 'fsdp', 'tensor'), may hold values from -6 to 6
- segment_ids: int32 [8, 2048], P('dp'), may hold values from 0 to 7, never falling along the last dimension, each value on 1 to 1024 neighbouring positions
- blend: float32 [1], replicated, may hold values from 0.1 to 0.9
- w_first: bfloat16 [6144, 3072], P(('dp', 'fsdp'), 'tensor'), may hold values from -0.109375 to 0.109375
- w_second: bfloat16 [6144, 3072], P(('dp', 'fsdp'), 'tensor'), may hold values from -0.109375 to 0.109375
Outputs:
- mixed: bfloat16 [8, 2048, 6144], P('dp', 'fsdp', 'tensor')
The draws below stay inside these ranges and needn't reach their ends.
Inputs may be any that keep to these rules, and one draw needn't show every extreme that they name: `segment_ids`: within each pack image numbers never fall, each of the 8 images holds 1 to 1024 patches, and one holds exactly 1024.
All inputs are finite; a program needn't handle non-finite values.
Results may differ from the reference program's by a relative error of at most 0.012.
Values may be sent and summed in bfloat16 or wider, within the bound.
A program may use at most 64 MiB of HBM per device.

```python
import math
import jax
import jax.numpy as jnp
import numpy as np
from jax import lax

D = 6144
HEADS = 24
HEAD_DIM = 128
IMAGES = 8
HQ = 3072
PACK = 2048
MOST = 1024
N_DP = 8
N_TENSOR = 4


def draw_query(key, part):
    key = jax.random.fold_in(key, 11)
    first = jax.random.fold_in(key, 0)
    result = jnp.clip(1.5 * jax.random.normal(first, (N_DP, PACK, HQ), jnp.float32), -9.0, 9.0)
    return result.astype(jnp.bfloat16)


def draw_key_in(key, part):
    key = jax.random.fold_in(key, 12)
    noise = jax.random.normal(key, (N_DP, PACK, HQ), jnp.float32)
    result = jnp.clip(1.5 * noise, -9.0, 9.0)
    return result.astype(jnp.bfloat16)


def steps_of(stream_key, extent, cuts, low, top_value):
    level, own = 1.0, jax.random.fold_in(stream_key, 6)
    for dim, shards_of in cuts:
        heights = jnp.exp(jax.random.uniform(jax.random.fold_in(own, dim), (shards_of,), jnp.float32, low / len(cuts), top_value / len(cuts)))
        level = level * jnp.repeat(heights, extent[dim] // shards_of).reshape([-1 if axis == dim else 1 for axis in range(len(extent))])
    return level


def length_profile(amount, total, reach, skew):
    loads = [(1 << 20) // math.isqrt(rank ** skew) + 1 for rank in range(2, amount + 1)]
    rest, counts = total - reach - (amount - 1), [1] * (amount - 1)
    while rest > 0:
        movable = [i for i in range(amount - 1) if counts[i] < reach]
        whole, left = sum([loads[i] for i in movable]), rest
        for i in movable:
            more = min(reach - counts[i], max(1, left * loads[i] // whole), rest)
            counts[i] = counts[i] + more
            rest = rest - more
    return np.array([reach] + counts)


def uneven_parts(stream_key, count, total, bound, lean):
    if count == 2:
        one = jax.random.randint(stream_key, (), max(1, total - bound), min(bound, total - 1) + 1)
        return jnp.stack([one, total - one])
    tallies = jnp.asarray(length_profile(count, total, bound, lean), jnp.int32)
    twos = (count - 1) // 2
    source_of, receiver = tallies[1:1 + 2 * twos:2], tallies[2:2 + 2 * twos:2]
    room = jnp.minimum(source_of - 1, bound - receiver)
    shifted = jax.random.randint(jax.random.fold_in(stream_key, 1), (twos,), 0, 1 << 20) % (room + 1)
    tallies = tallies.at[1:1 + 2 * twos:2].set(source_of - shifted).at[2:2 + 2 * twos:2].set(receiver + shifted)
    return tallies[jax.random.permutation(jax.random.fold_in(stream_key, 2), count)]


def bell_draw(own_key, extent, spread, most, shards=(), held_as=jnp.bfloat16):
    drawn = jax.random.normal(own_key, extent, jnp.float32) * spread
    if len(shards) > 0:
        drawn = steps_of(own_key, extent, shards, -0.22, 0.18) * drawn
    return jnp.clip(drawn, min=-most, max=most).astype(held_as)


def setup_inputs(seed: int = 0) -> dict:
    arg_keys = jax.random.split(jax.random.key(seed), 8)
    query = draw_query(jax.random.fold_in(arg_keys[7], 71), 0)
    key_in = draw_key_in(jax.random.fold_in(arg_keys[7], 71), 0)
    value = bell_draw(arg_keys[2], (N_DP, PACK, HQ), 1.0, 6.0, ((0, 8), (1, 16), (2, 4)))
    segment_ids = jax.vmap(lambda own: jnp.searchsorted(jnp.cumsum(uneven_parts(own, IMAGES, PACK, MOST, 2)), jnp.arange(PACK), side="right"))(jax.random.split(arg_keys[3], N_DP)).reshape((N_DP, PACK)).astype(jnp.int32)
    blend = jnp.clip(jax.random.uniform(arg_keys[4], (1,), jnp.float32, 0.1, 0.9), 0.1, 0.9)
    w_first = bell_draw(arg_keys[5], (D, HQ), HQ ** -0.5, 0.109375, ((0, 128), (1, 4)))
    w_second = bell_draw(arg_keys[6], (D, HQ), HQ ** -0.5, 0.109375, ((0, 128), (1, 4)))
    return dict(query=query, key_in=key_in, value=value, segment_ids=segment_ids, blend=blend, w_first=w_first, w_second=w_second)


def attend_pack(query, key_in, value, segs):
    same = segs[:, None] == segs[None, :]
    qh = query.reshape(PACK, HEADS, HEAD_DIM).transpose(1, 0, 2)
    kh = key_in.reshape(PACK, HEADS, HEAD_DIM).transpose(1, 0, 2)
    vh = value.reshape(PACK, HEADS, HEAD_DIM).transpose(1, 0, 2)

    def one_head(items):
        qa, ka, va = items
        scores = jnp.dot(qa, ka.T, preferred_element_type=jnp.float32) * (HEAD_DIM ** -0.5)
        scores = jnp.where(same, scores, jnp.float32(-1e30))
        top = jnp.max(scores, axis=1, keepdims=True)
        expo = jnp.exp(scores - top)
        probs = (expo / jnp.sum(expo, axis=1, keepdims=True)).astype(jnp.bfloat16)
        return jnp.dot(probs, va, preferred_element_type=jnp.float32).astype(jnp.bfloat16)

    heads_out = lax.map(one_head, (qh, kh, vh))
    return heads_out.transpose(1, 0, 2).reshape(PACK, HQ)


def reference(query, key_in, value, segment_ids, blend, w_first, w_second):
    coef = blend[0]
    weight = ((1.0 - coef) * w_first.astype(jnp.float32) + coef * w_second.astype(jnp.float32)).astype(jnp.bfloat16)
    group = HQ // N_TENSOR

    def one_pack(items):
        qa, ka, va, segs = items
        attended = attend_pack(qa, ka, va, segs)
        total = jnp.zeros((PACK, D), jnp.float32)
        for index in range(N_TENSOR):
            cols = attended[:, index * group:(index + 1) * group]
            rows_w = weight[:, index * group:(index + 1) * group]
            partial_value = jnp.dot(cols, rows_w.T, preferred_element_type=jnp.float32).astype(jnp.bfloat16)
            total = total + partial_value.astype(jnp.float32)
        return total.astype(jnp.bfloat16)

    return lax.map(one_pack, (query, key_in, value, segment_ids))
```

```python
import functools
import heapq

import jax
import jax.numpy as jnp
from jax import lax
from jax.experimental import pallas as pl
from jax.experimental.pallas import tpu as pltpu
from jax.sharding import PartitionSpec as P

HEAD_DIM = 128
MESH = pl.DeviceIdType.MESH
NT = (((1,), (1,)), ((), ()))


class Node:
    def __init__(self, name, deps, cost, link=None, rank=0):
        self.name, self.deps, self.cost, self.link, self.rank = name, list(deps), cost, link, rank


def order_of(nodes, latency=1.5):
    by_name = {node.name: node for node in nodes}
    position = {node.name: i for i, node in enumerate(nodes)}
    feeds = {node.name: False for node in nodes}
    for node in nodes:
        if node.link is not None:
            for dep in node.deps:
                feeds[dep] = True
    done, started, waited = set(), set(), set()
    arrivals, free, order, now = [], {}, [], 0.0
    while len(done) < len(nodes):
        for node in nodes:
            if node.link is not None and node.name not in started and all(d in done for d in node.deps):
                for d in node.deps:
                    if by_name[d].link is not None and d not in waited:
                        waited.add(d)
                        order.append(("wait", d))
                started.add(node.name)
                order.append(("start", node.name))
                begin = max(now, free.get(node.link, 0.0))
                free[node.link] = begin + node.cost
                heapq.heappush(arrivals, (begin + node.cost + latency, position[node.name], node.name))
        if arrivals and arrivals[0][0] <= now:
            name = heapq.heappop(arrivals)[2]
            done.add(name)
            if feeds[name] and name not in waited:
                waited.add(name)
                order.append(("wait", name))
            continue
        ready = [n for n in nodes if n.link is None and n.name not in done and all(d in done for d in n.deps)]
        if ready:
            node = min(ready, key=lambda n: (n.rank, position[n.name]))
            for d in node.deps:
                if by_name[d].link is not None and d not in waited:
                    waited.add(d)
                    order.append(("wait", d))
            order.append(("compute", node.name))
            now += node.cost
            done.add(node.name)
            continue
        now = max(now, arrivals[0][0])
    return order


def plan(n_y, n_z, heads):
    nodes = []

    def add(name, deps, cost, link=None, rank=0):
        nodes.append(Node(name, deps, cost, link, rank))
        return name

    w_cost, kv_cost = 1.5, 2.0
    offsets = [0]
    for k in range(1, n_y // 2 + 1):
        offsets += [-k, k] if 2 * k < n_y else [-k]
    add(("blend",), [], 0.3, rank=-3)
    for j in offsets:
        if j == 0:
            continue
        link = "y+" if j < 0 else "y-"
        sign = 1 if j > 0 else -1
        add(("wy", j), [("wy", j - sign)] if abs(j) > 1 else [("blend",)], w_cost, link)
    for slot, j in enumerate(offsets):
        source = ("wy", j) if j else ("blend",)
        up = n_z // 2 - (slot % 2)
        for k in range(1, n_z // 2 + 1):
            for way, most in ((1, up), (-1, n_z - 1 - up)):
                if k <= most:
                    link = "z+" if way > 0 else "z-"
                    add(("wz", slot, way * k), [("wz", slot, way * (k - 1))] if k > 1 else [source], w_cost, link)
    add(("local",), [], 0.5, rank=-2)
    for part in ("k", "v", "q"):
        add(("x", part), [], kv_cost, "x")
    for part, up in (("k", n_y // 2), ("v", n_y - 1 - n_y // 2)):
        for own in (1, 0):
            source = ("local",) if own else ("x", part)
            for k in range(1, n_y // 2 + 1):
                for way, most in ((1, up), (-1, n_y - 1 - up)):
                    if k <= most:
                        link = "y+" if way > 0 else "y-"
                        add((part, own, way * k), [(part, own, way * (k - 1))] if k > 1 else [source], kv_cost, link)
    add(("mask",), [], 1.0, rank=-1)
    held = [("mask",), ("local",)] + [n.name for n in nodes if n.name[0] in ("k", "v", "x")]
    for h in range(heads):
        for half in range(2):
            add(("attn", h, half), held, 0.8)
        add(("a", h), [("attn", h, 0), ("attn", h, 1)], 1.3, "x")
    ready = [("a", h) for h in range(heads)]
    for slot, j in enumerate(offsets):
        shards = [n.name for n in nodes if n.name[0] == "wz" and n.name[1] == slot]
        source = ("wy", j) if j else ("blend",)
        add(("proj", slot), ready + shards + [source], 0.4, rank=slot)
        add(("c", slot), [("proj", slot)], 0.3, "core")
        add(("add", slot), [("c", slot)], 0.1, rank=slot - 20)
        for r in range(3):
            add(("e", slot, r), [("add", slot)], 0.5 if r else 1.0, "x")
        add(("sum", slot), [("e", slot, r) for r in range(3)], 0.1, rank=slot + 20)
    add(("last",), [("sum", slot) for slot in range(n_y)], 0.5, rank=100)
    return nodes, offsets


def kernel(
    n_y, n_z, order, ids, offsets,
    q_hbm, k_hbm, v_hbm, seg_ref, blend_ref, w_first, w_second, out_ref,
    kbuf, vbuf, qbuf, bias, wbuf, attbuf, p_own, p_send, c_recv, s_send, s_keep, e_recv, out_t,
    local_sem, send_sem, recv_sem,
):
    z = lax.axis_index("dp")
    f = lax.axis_index("fsdp")
    t = lax.axis_index("tensor")
    y, x = f // 2, f % 2
    x_hi, core = t // 2, t % 2
    rows = q_hbm.shape[1]
    half_width = kbuf.shape[1]
    heads = half_width // HEAD_DIM
    piece = w_first.shape[0]
    x_other = f + 1 - 2 * x
    t_core = t + 1 - 2 * core
    t_hi = t + 2 - 4 * x_hi

    def y_at(d):
        return (y + d + 2 * n_y) % n_y

    def z_at(d):
        return (z + d + 2 * n_z) % n_z

    def to(dp=None, fsdp=None, tensor=None):
        return (z if dp is None else dp, f if fsdp is None else fsdp, t if tensor is None else tensor)

    partners = [
        to(fsdp=x_other),
        to(tensor=t_core),
        to(tensor=t_hi),
        to(fsdp=x_other, tensor=t_hi),
        to(fsdp=y_at(1) * 2 + x),
        to(fsdp=y_at(-1) * 2 + x),
        to(dp=z_at(1)),
        to(dp=z_at(-1)),
    ]

    mine = pl.ds(pl.multiple_of(x * half_width, HEAD_DIM), half_width)
    theirs = pl.ds(pl.multiple_of((1 - x) * half_width, HEAD_DIM), half_width)

    def token_rows(y_index, x_index):
        return pl.ds(pl.multiple_of((y_index * 2 + x_index) * rows, rows), rows)

    bufs = {"k": kbuf, "v": vbuf, "q": qbuf}
    hbm = {"k": k_hbm, "v": v_hbm, "q": q_hbm}

    def q_rows(x_index):
        return pl.ds(pl.multiple_of(x_index * rows, rows), rows)

    locals_ = []
    for i, part in enumerate(("k", "v", "q")):
        at = q_rows(x) if part == "q" else token_rows(y, x)
        locals_.append(pltpu.make_async_copy(hbm[part].at[0, :, mine], bufs[part].at[at], local_sem.at[i]))
    for copy in locals_:
        copy.start()

    barrier = pltpu.get_barrier_semaphore()
    for partner in partners:
        pl.semaphore_signal(barrier, inc=1, device_id=partner, device_id_type=MESH)
    pl.semaphore_wait(barrier, len(partners))

    def copy_of(name, arriving):
        kind = name[0]
        if kind == "wy":
            j = name[1]
            sign = 1 if j > 0 else -1
            src = dst = wbuf.at[y_at(j if arriving else j - sign), z]
            who = to(fsdp=y_at(-sign) * 2 + x)
        elif kind == "wz":
            slot, k = name[1:]
            way = 1 if k > 0 else -1
            src = dst = wbuf.at[y_at(offsets[slot]), z_at(-k if arriving else -(k - way))]
            who = to(dp=z_at(way))
        elif kind == "x":
            part = name[1]
            from_x = 1 - x if arriving else x
            at = q_rows(from_x) if part == "q" else token_rows(y, from_x)
            dst = bufs[part].at[at]
            src = dst if arriving else hbm[part].at[0, :, theirs]
            who = to(fsdp=x_other)
        elif kind in ("k", "v"):
            own, k = name[1:]
            way = 1 if k > 0 else -1
            part_x = x if own else 1 - x
            src = dst = bufs[kind].at[token_rows(y_at(-k if arriving else -(k - way)), part_x)]
            who = to(fsdp=y_at(way) * 2 + x)
        elif kind == "a":
            h = name[1]
            src = dst = attbuf.at[((1 - x) if arriving else x) * heads + h]
            who = to(fsdp=x_other)
        elif kind == "c":
            slot = name[1]
            dst = c_recv.at[slot]
            src = dst if arriving else p_send.at[slot]
            who = to(tensor=t_core)
        else:
            slot, r = name[1:]
            dst = e_recv.at[r, slot]
            src = dst if arriving else s_send.at[r, slot]
            who = partners[(2, 3, 0)[r]]
        i = ids[name]
        return pltpu.make_async_remote_copy(
            src_ref=src, dst_ref=dst, send_sem=send_sem.at[i], recv_sem=recv_sem.at[i],
            device_id=who, device_id_type=MESH,
        )

    def blend():
        coef = blend_ref[0]
        mixed = (1.0 - coef) * w_first[...].astype(jnp.float32) + coef * w_second[...].astype(jnp.float32)
        wbuf[y, z] = mixed.astype(jnp.bfloat16)

    def mask():
        count = 2 * rows
        row = seg_ref[:, pl.ds(pl.multiple_of(y * count, count), count)].astype(jnp.float32)
        on = lax.broadcasted_iota(jnp.int32, (count, count), 0) == lax.broadcasted_iota(jnp.int32, (count, count), 1)
        column = jnp.sum(jnp.where(on, jnp.broadcast_to(row, (count, count)), 0.0), axis=1, keepdims=True)
        keys = seg_ref[...].astype(jnp.float32)
        bias[...] = jnp.where(column == keys, jnp.float32(0.0), jnp.float32(-1e30))

    def attn(h, half):
        at, cols = slice(half * rows, (half + 1) * rows), slice(h * HEAD_DIM, (h + 1) * HEAD_DIM)
        scores = lax.dot_general(qbuf[at, cols], kbuf[:, cols], NT, preferred_element_type=jnp.float32)
        scores = scores * HEAD_DIM ** (-0.5) + bias[at, :]
        top = jnp.max(scores, axis=1, keepdims=True)
        expo = jnp.exp(scores - top)
        total = jnp.sum(expo, axis=1, keepdims=True)
        result = jnp.dot(expo.astype(jnp.bfloat16), vbuf[:, cols], preferred_element_type=jnp.float32)
        attbuf[x * heads + h, at, :] = (result / total).astype(jnp.bfloat16)

    def proj(slot):
        attended = jnp.concatenate([attbuf[i] for i in range(2 * heads)], axis=1)
        shards = wbuf.at[y_at(offsets[slot])]
        per = n_z // 4
        for hi in range(2):
            for same in range(2):
                first = (hi * 2 + (core if same else 1 - core)) * per
                weight = shards[pl.ds(first, per)].reshape(per * piece, attended.shape[1])
                part = lax.dot_general(weight, attended, NT, preferred_element_type=jnp.float32).astype(jnp.bfloat16)
                (p_own if same else p_send)[slot, hi] = part

    def add(slot):
        for away in range(2):
            hi = (1 - x_hi) if away else x_hi
            both = (p_own[slot, hi].astype(jnp.float32) + c_recv[slot, hi].astype(jnp.float32)).astype(jnp.bfloat16)
            first, second = both[:, :rows], both[:, rows:]
            keep = jnp.where(x == 0, first, second)
            move = jnp.where(x == 0, second, first)
            if away:
                s_send[0, slot] = keep
                s_send[1, slot] = move
            else:
                s_keep[slot] = keep
                s_send[2, slot] = move

    def total(slot):
        at = y_at(offsets[slot])
        per = n_z // 4
        own = s_keep[slot].astype(jnp.float32) + e_recv[0, slot].astype(jnp.float32)
        other = e_recv[1, slot].astype(jnp.float32) + e_recv[2, slot].astype(jnp.float32)
        for i in range(per):
            part = slice(i * piece, (i + 1) * piece)
            out_t[i, at, x] = own[part].astype(jnp.bfloat16)
            out_t[i, at, 1 - x] = other[part].astype(jnp.bfloat16)

    def last():
        eye = lax.broadcasted_iota(jnp.int32, (rows, rows), 0) == lax.broadcasted_iota(jnp.int32, (rows, rows), 1)
        eye = jnp.where(eye, 1.0, 0.0).astype(jnp.bfloat16)
        flat = out_t[...].reshape(out_ref.shape[2], rows)
        out_ref[0] = lax.dot_general(eye, flat, NT, preferred_element_type=jnp.float32).astype(jnp.bfloat16)

    def local():
        for copy in locals_:
            copy.wait()

    work = {
        "blend": blend, "mask": mask, "attn": attn, "proj": proj, "add": add, "sum": total, "last": last, "local": local,
    }
    for verb, name in order:
        if verb == "start":
            copy_of(name, False).start()
        elif verb == "wait":
            copy_of(name, True).wait_recv()
        else:
            work[name[0]](*name[1:])
    for name in ids:
        copy_of(name, False).wait_send()


def per_device(n_y, n_z, query, key_in, value, segment_ids, blend, w_first, w_second):
    rows, width = query.shape[1], query.shape[2]
    heads = width // HEAD_DIM // 2
    half = width // 2
    patches = segment_ids.shape[1]
    piece = w_first.shape[0]
    nodes, offsets = plan(n_y, n_z, heads)
    order = order_of(nodes)
    ids = {}
    for node in nodes:
        if node.link is not None:
            ids[node.name] = len(ids)
    bf16, f32 = jnp.bfloat16, jnp.float32
    group = n_z // 4 * piece
    any_, vmem = pl.BlockSpec(memory_space=pl.ANY), pl.BlockSpec(memory_space=pltpu.VMEM)
    out_cols = 2 * n_y * group
    return pl.pallas_call(
        functools.partial(kernel, n_y, n_z, order, ids, offsets),
        out_shape=jax.ShapeDtypeStruct((1, rows, out_cols), bf16),
        in_specs=[any_, any_, any_, vmem, pl.BlockSpec(memory_space=pltpu.SMEM), vmem, vmem],
        out_specs=vmem,
        scratch_shapes=[
            pltpu.VMEM((patches, half), bf16),
            pltpu.VMEM((patches, half), bf16),
            pltpu.VMEM((2 * rows, half), bf16),
            pltpu.VMEM((2 * rows, patches), f32),
            pltpu.VMEM((n_y, n_z, piece, width), bf16),
            pltpu.VMEM((2 * heads, 2 * rows, HEAD_DIM), bf16),
            pltpu.VMEM((n_y, 2, group, 2 * rows), bf16),
            pltpu.VMEM((n_y, 2, group, 2 * rows), bf16),
            pltpu.VMEM((n_y, 2, group, 2 * rows), bf16),
            pltpu.VMEM((3, n_y, group, rows), bf16),
            pltpu.VMEM((n_y, group, rows), bf16),
            pltpu.VMEM((3, n_y, group, rows), bf16),
            pltpu.VMEM((n_z // 4, n_y, 2, piece, rows), bf16),
            pltpu.SemaphoreType.DMA((3,)),
            pltpu.SemaphoreType.DMA((len(ids),)),
            pltpu.SemaphoreType.DMA((len(ids),)),
        ],
        compiler_params=pltpu.CompilerParams(
            collective_id=0, has_side_effects=True, vmem_limit_bytes=48 * 1024 * 1024
        ),
    )(query, key_in, value, segment_ids, blend, w_first, w_second)


def solution(mesh):
    in_specs = (
        P("dp", "fsdp", "tensor"),
        P("dp", "fsdp", "tensor"),
        P("dp", "fsdp", "tensor"),
        P("dp", None),
        P(),
        P(("dp", "fsdp"), "tensor"),
        P(("dp", "fsdp"), "tensor"),
    )
    out_specs = P("dp", "fsdp", "tensor")
    body = functools.partial(per_device, mesh.shape["fsdp"] // 2, mesh.shape["dp"])
    return jax.shard_map(body, mesh=mesh, in_specs=in_specs, out_specs=out_specs, check_vma=False)
```

```python
import functools
import heapq

import jax
import jax.numpy as jnp
from jax import lax
from jax.experimental import pallas as pl
from jax.experimental.pallas import tpu as pltpu
from jax.sharding import PartitionSpec as P

HEAD_DIM = 128
LAST = 256
IDLE = 4
WINDOW = 6
MESH = pl.DeviceIdType.MESH
NT = (((1,), (1,)), ((), ()))


class Node:
    def __init__(self, name, deps, cost, link=None, rank=0):
        self.name, self.deps, self.cost, self.link, self.rank = name, list(deps), cost, link, rank


def order_of(nodes, latency=2.0):
    by_name = {node.name: node for node in nodes}
    position = {node.name: i for i, node in enumerate(nodes)}
    feeds = {node.name: False for node in nodes}
    for node in nodes:
        if node.link is not None:
            for dep in node.deps:
                feeds[dep] = True
    done, started, waited = set(), set(), set()
    arrivals, free, order, now = [], {}, [], 0.0
    flying = []
    while len(done) < len(nodes):
        for node in nodes:
            if node.link is not None and node.name not in started and all(d in done for d in node.deps):
                for d in node.deps:
                    if by_name[d].link is not None and d not in waited:
                        waited.add(d)
                        order.append(("wait", d))
                started.add(node.name)
                order.append(("start", node.name))
                begin = max(now, free.get(node.link, 0.0))
                free[node.link] = begin + node.cost
                heapq.heappush(arrivals, (begin + node.cost + latency, position[node.name], node.name))
                flying.append((begin + node.cost + latency, node.name))
        if arrivals and arrivals[0][0] <= now:
            name = heapq.heappop(arrivals)[2]
            done.add(name)
            if feeds[name] and name not in waited:
                waited.add(name)
                order.append(("wait", name))
            continue
        ready = [n for n in nodes if n.link is None and n.name not in done and all(d in done for d in n.deps)]
        if ready:
            node = min(ready, key=lambda n: (n.rank, position[n.name]))
            for d in node.deps:
                if by_name[d].link is not None and d not in waited:
                    waited.add(d)
                    order.append(("wait", d))
            order.append(("compute", node.name))
            now += node.cost
            done.add(node.name)
            continue
        for item in sorted(flying)[:IDLE]:
            if item[0] + 1.0 < now:
                flying.remove(item)
                order.append(("sent", item[1]))
        now = max(now, arrivals[0][0])
    return order + [("sent", name) for _, name in sorted(flying)]


def plan(n_y, n_z, heads):
    nodes = []

    def add(name, deps, cost, link=None, rank=0):
        nodes.append(Node(name, deps, cost, link, rank))
        return name

    w_cost, kv_cost = 1.6, 1.4
    offsets = [0]
    for k in range(1, n_y // 2 + 1):
        offsets += [-k, k] if 2 * k < n_y else [-k]
    add(("blend",), [], 0.3, rank=-3)
    for j in offsets:
        if j == 0:
            continue
        link = "y+" if j < 0 else "y-"
        sign = 1 if j > 0 else -1
        add(("wy", j), [("wy", j - sign)] if abs(j) > 1 else [("blend",)], w_cost, link)
    for slot, j in enumerate(offsets):
        source = ("wy", j) if j else ("blend",)
        cost = w_cost * (1 - LAST / 768 if abs(j) == 1 else 1)
        up = n_z // 2 - (slot % 2)
        for k in range(1, n_z // 2 + 1):
            for way, most in ((1, up), (-1, n_z - 1 - up)):
                if k <= most:
                    link = "z+" if way > 0 else "z-"
                    add(("wz", slot, way * k), [("wz", slot, way * (k - 1))] if k > 1 else [source], cost, link)
    add(("local",), [], 0.5, rank=-2)
    for h in range(heads):
        for i in range(2):
            add(("x", h, i), [], kv_cost / 2, "x")
    add(("xq",), [], kv_cost, "x")
    streams = [(h, own) for h in range(heads) for own in (1, 0)]
    hops = {1: (n_y // 2, n_y - 1 - n_y // 2), 0: (n_y - 1 - n_y // 2, n_y // 2)}
    for i, (h, own) in enumerate(streams):
        source = [("local",)] if own else [("x", h, 0), ("x", h, 1)]
        for k in range(1, n_y // 2 + 1):
            for way, most in zip((1, -1), hops[own]):
                if k <= most:
                    deps = [("kv", h, own, way * (k - 1))] if k > 1 else list(source)
                    if k == 1 and i >= WINDOW:
                        before = streams[i - WINDOW]
                        deps.append(("kv", *before, way * (hops[before[1]][way < 0] - 1)))
                    add(("kv", h, own, way * k), deps, kv_cost, "y+" if way > 0 else "y-")
    if LAST:
        gathered = [n.name for n in nodes if n.name[:2] == ("wz", 0)]
        for j in (-1, 1):
            late = [("kv", h, own, -j * hops[own][j > 0]) for h, own in streams]
            add(("yl", j), gathered + late, 13.0 * LAST / 768, "y+" if j < 0 else "y-")
    add(("mask",), [], 1.0, rank=-1)
    for h in range(heads):
        held = [("mask",), ("local",), ("x", h, 0), ("x", h, 1), ("xq",)]
        rest = [n.name for n in nodes if n.name[:2] == ("kv", h) and 2 * abs(n.name[3]) == n_y]
        held += [n.name for n in nodes if n.name[:2] == ("kv", h) and 2 * abs(n.name[3]) < n_y]
        for half in range(2):
            add(("near", h, half), held, 0.5)
            add(("far", h, half), [("near", h, half)] + rest, 0.15, rank=-5)
            add(("a", h, half), [("far", h, half)], 0.7, "x")
    ready = [("a", h, half) for h in range(heads) for half in range(2)]
    for slot, j in enumerate(offsets):
        shards = [n.name for n in nodes if n.name[0] == "wz" and n.name[1] == slot]
        source = [("wy", j)] if j else [("blend",)]
        if LAST and abs(j) == 1:
            source.append(("yl", j))
        add(("pre", slot), ready[:-2] + shards + source, 0.35, rank=slot + 30)
        add(("proj", slot), ready[-2:] + [("pre", slot)], 0.2, rank=slot)
        add(("c", slot), [("proj", slot)], 0.3, "core")
        add(("add", slot), [("c", slot)], 0.1, rank=slot - 20)
        for r in range(3):
            add(("e", slot, r), [("add", slot)], 1.0, "x%d" % r)
        add(("sum", slot), [("e", slot, r) for r in range(3)], 0.1, rank=slot + 20)
    add(("last",), [("sum", slot) for slot in range(n_y)], 0.5, rank=100)
    return nodes, offsets


def kernel(
    n_y, n_z, order, ids, offsets,
    q_hbm, k_hbm, v_hbm, seg_ref, blend_ref, w_first, w_second, out_ref,
    kvbuf, qbuf, bias, stats, wbuf, attbuf, acc, p_all, c_recv, s_send, s_keep, e_recv, out_t,
    local_sem, send_sem, recv_sem,
):
    z = lax.axis_index("dp")
    f = lax.axis_index("fsdp")
    t = lax.axis_index("tensor")
    y, x = f // 2, f % 2
    x_hi, core = t // 2, t % 2
    rows = q_hbm.shape[1]
    half_width = q_hbm.shape[2] // 2
    heads = half_width // HEAD_DIM
    piece = w_first.shape[0]
    split = w_first.shape[1] - LAST
    x_other = f + 1 - 2 * x
    t_core = t + 1 - 2 * core
    t_hi = t + 2 - 4 * x_hi

    ys = [(y + d) % n_y for d in range(n_y)]
    zs = [(z + d) % n_z for d in range(n_z)]

    def y_at(d):
        return ys[d % n_y]

    def z_at(d):
        return zs[d % n_z]

    def to(dp=None, fsdp=None, tensor=None):
        return (z if dp is None else dp, f if fsdp is None else fsdp, t if tensor is None else tensor)

    partners = [
        to(fsdp=x_other),
        to(tensor=t_core),
        to(tensor=t_hi),
        to(fsdp=x_other, tensor=t_hi),
        to(fsdp=y_at(1) * 2 + x),
        to(fsdp=y_at(-1) * 2 + x),
        to(dp=z_at(1)),
        to(dp=z_at(-1)),
    ]

    mine = pl.ds(pl.multiple_of(x * half_width, HEAD_DIM), half_width)
    theirs = pl.ds(pl.multiple_of((1 - x) * half_width, HEAD_DIM), half_width)

    def token_rows(y_index, x_index):
        return pl.ds(pl.multiple_of((y_index * 2 + x_index) * rows, rows), rows)

    def head_of(x_index, h):
        return pl.ds(pl.multiple_of((x_index * heads + h) * HEAD_DIM, HEAD_DIM), HEAD_DIM)

    def q_rows(x_index):
        return pl.ds(pl.multiple_of(x_index * rows, rows), rows)

    locals_ = [pltpu.make_async_copy(q_hbm.at[0, :, mine], qbuf.at[q_rows(x)], local_sem.at[0])]
    for h in range(heads):
        for i, source in enumerate((k_hbm, v_hbm)):
            locals_.append(
                pltpu.make_async_copy(
                    source.at[0, :, head_of(x, h)], kvbuf.at[h, i, token_rows(y, x)], local_sem.at[1 + 2 * h + i]
                )
            )
    for copy in locals_:
        copy.start()

    barrier = pltpu.get_barrier_semaphore()
    for partner in partners:
        pl.semaphore_signal(barrier, inc=1, device_id=partner, device_id_type=MESH)
    pl.semaphore_wait(barrier, len(partners))

    def copy_of(name, arriving):
        kind = name[0]
        if kind == "wy":
            j = name[1]
            sign = 1 if j > 0 else -1
            src = dst = wbuf.at[y_at(j if arriving else j - sign), z]
            who = to(fsdp=y_at(-sign) * 2 + x)
        elif kind == "wz":
            slot, k = name[1:]
            way = 1 if k > 0 else -1
            src = dst = wbuf.at[y_at(offsets[slot]), z_at(-k if arriving else -(k - way))]
            if abs(offsets[slot]) == 1 and LAST:
                src = dst = src.at[:, :split]
            who = to(dp=z_at(way))
        elif kind == "yl":
            j = name[1]
            src = dst = wbuf.at[y_at(j if arriving else 0), :, :, split:]
            who = to(fsdp=y_at(-j) * 2 + x)
        elif kind == "xq":
            dst = qbuf.at[q_rows(1 - x if arriving else x)]
            src = dst if arriving else q_hbm.at[0, :, theirs]
            who = to(fsdp=x_other)
        elif kind == "x":
            h, i = name[1:]
            dst = kvbuf.at[h, i, token_rows(y, 1 - x if arriving else x)]
            src = dst if arriving else (k_hbm, v_hbm)[i].at[0, :, head_of(1 - x, h)]
            who = to(fsdp=x_other)
        elif kind == "kv":
            h, own, k = name[1:]
            way = 1 if k > 0 else -1
            part_x = x if own else 1 - x
            src = dst = kvbuf.at[h, :, token_rows(y_at(-k if arriving else -(k - way)), part_x)]
            who = to(fsdp=y_at(way) * 2 + x)
        elif kind == "a":
            h, half = name[1:]
            src = dst = attbuf.at[((1 - x) if arriving else x) * heads + h, half * rows : (half + 1) * rows]
            who = to(fsdp=x_other)
        elif kind == "c":
            slot = name[1]
            dst = c_recv.at[slot]
            src = dst if arriving else p_all.at[slot, :, 1 - core]
            who = to(tensor=t_core)
        else:
            slot, r = name[1:]
            dst = e_recv.at[r, slot]
            src = dst if arriving else s_send.at[r, slot]
            who = partners[(2, 3, 0)[r]]
        i = ids[name]
        return pltpu.make_async_remote_copy(
            src_ref=src, dst_ref=dst, send_sem=send_sem.at[i], recv_sem=recv_sem.at[i],
            device_id=who, device_id_type=MESH,
        )

    def blend():
        coef = blend_ref[0]
        mixed = (1.0 - coef) * w_first[...].astype(jnp.float32) + coef * w_second[...].astype(jnp.float32)
        wbuf[y, z] = mixed.astype(jnp.bfloat16)

    def mask():
        count = 2 * rows
        row = seg_ref[:, pl.ds(pl.multiple_of(y * count, count), count)].astype(jnp.float32)
        on = lax.broadcasted_iota(jnp.int32, (count, count), 0) == lax.broadcasted_iota(jnp.int32, (count, count), 1)
        column = jnp.sum(jnp.where(on, jnp.broadcast_to(row, (count, count)), 0.0), axis=1, keepdims=True)
        keys = seg_ref[...].astype(jnp.float32)
        bias[...] = jnp.where(column == keys, jnp.float32(0.0), jnp.float32(-1e30))

    def scores_of(h, half, j):
        at, cols = slice(half * rows, (half + 1) * rows), slice(h * HEAD_DIM, (h + 1) * HEAD_DIM)
        keys = pl.ds(pl.multiple_of(y_at(j) * 2 * rows, 2 * rows), 2 * rows)
        scores = lax.dot_general(qbuf[at, cols], kvbuf[h, 0, keys], NT, preferred_element_type=jnp.float32)
        return scores * HEAD_DIM ** (-0.5) + bias[at, keys], keys

    def near(h, half):
        blocks = [scores_of(h, half, j) for j in range(1 - n_y // 2, n_y // 2)]
        top = jnp.max(functools.reduce(jnp.maximum, [scores for scores, _ in blocks]), axis=1, keepdims=True)
        expos = [jnp.exp(scores - top) for scores, _ in blocks]
        total = jnp.sum(functools.reduce(jnp.add, expos), axis=1, keepdims=True)
        result = jnp.zeros((rows, HEAD_DIM), jnp.float32)
        for expo, (_, keys) in zip(expos, blocks):
            result += jnp.dot(expo.astype(jnp.bfloat16), kvbuf[h, 1, keys], preferred_element_type=jnp.float32)
        stats[h, half, 0] = jnp.broadcast_to(top, (rows, HEAD_DIM))
        stats[h, half, 1] = jnp.broadcast_to(total, (rows, HEAD_DIM))
        stats[h, half, 2] = result

    def far(h, half):
        scores, keys = scores_of(h, half, n_y // 2)
        before = stats[h, half, 0][:, :1]
        top = jnp.maximum(before, jnp.max(scores, axis=1, keepdims=True))
        expo, shrink = jnp.exp(scores - top), jnp.exp(before - top)
        total = stats[h, half, 1][:, :1] * shrink + jnp.sum(expo, axis=1, keepdims=True)
        result = jnp.dot(expo.astype(jnp.bfloat16), kvbuf[h, 1, keys], preferred_element_type=jnp.float32)
        result = (stats[h, half, 2] * shrink + result) / total
        attbuf[x * heads + h, half * rows : (half + 1) * rows, :] = result.astype(jnp.bfloat16)

    def product(slot, spans):
        at = y_at(offsets[slot])
        weight = jnp.concatenate(
            [wbuf[at, :, :, a * HEAD_DIM : b * HEAD_DIM].reshape(n_z * piece, (b - a) * HEAD_DIM) for a, b in spans], axis=1
        )
        attended = jnp.concatenate([attbuf[i] for a, b in spans for i in range(a, b)], axis=1)
        return lax.dot_general(weight, attended, NT, preferred_element_type=jnp.float32)

    def pre(slot):
        acc[slot] = product(slot, [(0, heads - 1), (heads, 2 * heads - 1)])

    def proj(slot):
        part = acc[slot] + product(slot, [(heads - 1, heads), (2 * heads - 1, 2 * heads)])
        p_all[slot] = part.astype(jnp.bfloat16).reshape(p_all.shape[1:])

    def add(slot):
        for away in range(2):
            hi = (1 - x_hi) if away else x_hi
            both = (p_all[slot, hi, core].astype(jnp.float32) + c_recv[slot, hi].astype(jnp.float32)).astype(jnp.bfloat16)
            first, second = both[:, :rows], both[:, rows:]
            keep = jnp.where(x == 0, first, second)
            move = jnp.where(x == 0, second, first)
            if away:
                s_send[0, slot] = keep
                s_send[1, slot] = move
            else:
                s_keep[slot] = keep
                s_send[2, slot] = move

    def total(slot):
        at = y_at(offsets[slot])
        per = n_z // 4
        own = s_keep[slot].astype(jnp.float32) + e_recv[0, slot].astype(jnp.float32)
        other = e_recv[1, slot].astype(jnp.float32) + e_recv[2, slot].astype(jnp.float32)
        for i in range(per):
            part = slice(i * piece, (i + 1) * piece)
            out_t[i, at, x] = own[part].astype(jnp.bfloat16)
            out_t[i, at, 1 - x] = other[part].astype(jnp.bfloat16)

    def last():
        eye = lax.broadcasted_iota(jnp.int32, (rows, rows), 0) == lax.broadcasted_iota(jnp.int32, (rows, rows), 1)
        eye = jnp.where(eye, 1.0, 0.0).astype(jnp.bfloat16)
        flat = out_t[...].reshape(out_ref.shape[2], rows)
        out_ref[0] = lax.dot_general(eye, flat, NT, preferred_element_type=jnp.float32).astype(jnp.bfloat16)

    def local():
        for copy in locals_:
            copy.wait()

    work = {
        "blend": blend, "mask": mask, "near": near, "far": far, "pre": pre, "proj": proj, "add": add, "sum": total, "last": last, "local": local,
    }
    for verb, name in order:
        if verb == "start":
            copy_of(name, False).start()
        elif verb == "wait":
            copy_of(name, True).wait_recv()
        elif verb == "sent":
            copy_of(name, False).wait_send()
        else:
            work[name[0]](*name[1:])


def per_device(n_y, n_z, query, key_in, value, segment_ids, blend, w_first, w_second):
    rows, width = query.shape[1], query.shape[2]
    heads = width // HEAD_DIM // 2
    half = width // 2
    patches = segment_ids.shape[1]
    piece = w_first.shape[0]
    nodes, offsets = plan(n_y, n_z, heads)
    order = order_of(nodes)
    ids = {}
    for node in nodes:
        if node.link is not None:
            ids[node.name] = len(ids)
    bf16, f32 = jnp.bfloat16, jnp.float32
    group = n_z // 4 * piece
    any_, vmem = pl.BlockSpec(memory_space=pl.ANY), pl.BlockSpec(memory_space=pltpu.VMEM)
    out_cols = 2 * n_y * group
    return pl.pallas_call(
        functools.partial(kernel, n_y, n_z, order, ids, offsets),
        out_shape=jax.ShapeDtypeStruct((1, rows, out_cols), bf16),
        in_specs=[any_, any_, any_, vmem, pl.BlockSpec(memory_space=pltpu.SMEM), vmem, vmem],
        out_specs=vmem,
        scratch_shapes=[
            pltpu.VMEM((heads, 2, patches, HEAD_DIM), bf16),
            pltpu.VMEM((2 * rows, half), bf16),
            pltpu.VMEM((2 * rows, patches), f32),
            pltpu.VMEM((heads, 2, 3, rows, HEAD_DIM), f32),
            pltpu.VMEM((n_y, n_z, piece, width), bf16),
            pltpu.VMEM((2 * heads, 2 * rows, HEAD_DIM), bf16),
            pltpu.VMEM((n_y, n_z * piece, 2 * rows), f32),
            pltpu.VMEM((n_y, 2, 2, group, 2 * rows), bf16),
            pltpu.VMEM((n_y, 2, group, 2 * rows), bf16),
            pltpu.VMEM((3, n_y, group, rows), bf16),
            pltpu.VMEM((n_y, group, rows), bf16),
            pltpu.VMEM((3, n_y, group, rows), bf16),
            pltpu.VMEM((n_z // 4, n_y, 2, piece, rows), bf16),
            pltpu.SemaphoreType.DMA((1 + 2 * heads,)),
            pltpu.SemaphoreType.DMA((len(ids),)),
            pltpu.SemaphoreType.DMA((len(ids),)),
        ],
        compiler_params=pltpu.CompilerParams(
            collective_id=0, has_side_effects=True, vmem_limit_bytes=62 * 1024 * 1024
        ),
    )(query, key_in, value, segment_ids, blend, w_first, w_second)


def solution(mesh):
    in_specs = (
        P("dp", "fsdp", "tensor"),
        P("dp", "fsdp", "tensor"),
        P("dp", "fsdp", "tensor"),
        P("dp", None),
        P(),
        P(("dp", "fsdp"), "tensor"),
        P(("dp", "fsdp"), "tensor"),
    )
    out_specs = P("dp", "fsdp", "tensor")
    body = functools.partial(per_device, mesh.shape["fsdp"] // 2, mesh.shape["dp"])
    return jax.shard_map(body, mesh=mesh, in_specs=in_specs, out_specs=out_specs, check_vma=False)
```

```python
import functools
import heapq

import jax
import jax.numpy as jnp
from jax import lax
from jax.experimental import pallas as pl
from jax.experimental.pallas import tpu as pltpu
from jax.sharding import PartitionSpec as P

HEAD_DIM = 128
LAST = 256
IDLE = 4
WINDOW = 6
LATENCY, LATENCY_ELSE = {"y": 1.92, "z": 1.78}, 2.04
SHARD_US, BLOCK_US = 1.558, 1.335
MESH = pl.DeviceIdType.MESH
NT = (((1,), (1,)), ((), ()))


class Node:
    def __init__(self, name, deps, cost, link=None, rank=0):
        self.name, self.deps, self.cost, self.link, self.rank = name, list(deps), cost, link, rank


def order_of(nodes):
    by_name = {node.name: node for node in nodes}
    position = {node.name: i for i, node in enumerate(nodes)}
    feeds = {node.name: False for node in nodes}
    for node in nodes:
        if node.link is not None:
            for dep in node.deps:
                feeds[dep] = True
    done, started, waited = set(), set(), set()
    arrivals, free, order, now = [], {}, [], 0.0
    flying = []
    while len(done) < len(nodes):
        for node in nodes:
            if node.link is not None and node.name not in started and all(d in done for d in node.deps):
                for d in node.deps:
                    if by_name[d].link is not None and d not in waited:
                        waited.add(d)
                        order.append(("wait", d))
                started.add(node.name)
                order.append(("start", node.name))
                begin = max(now, free.get(node.link, 0.0))
                free[node.link] = begin + node.cost
                landing = begin + node.cost + LATENCY.get(node.link[0], LATENCY_ELSE)
                heapq.heappush(arrivals, (landing, position[node.name], node.name))
                flying.append((landing, node.name))
        if arrivals and arrivals[0][0] <= now:
            name = heapq.heappop(arrivals)[2]
            done.add(name)
            if feeds[name] and name not in waited:
                waited.add(name)
                order.append(("wait", name))
            continue
        ready = [n for n in nodes if n.link is None and n.name not in done and all(d in done for d in n.deps)]
        if ready:
            node = min(ready, key=lambda n: (n.rank, position[n.name]))
            for d in node.deps:
                if by_name[d].link is not None and d not in waited:
                    waited.add(d)
                    order.append(("wait", d))
            order.append(("compute", node.name))
            now += node.cost
            done.add(node.name)
            continue
        for item in sorted(flying)[:IDLE]:
            if item[0] + 1.0 < now:
                flying.remove(item)
                order.append(("sent", item[1]))
        now = max(now, arrivals[0][0])
    return order + [("sent", name) for _, name in sorted(flying)]


def plan(n_y, n_z, heads):
    nodes = []

    def add(name, deps, cost, link=None, rank=0):
        nodes.append(Node(name, deps, cost, link, rank))
        return name

    w_cost, kv_cost = SHARD_US, BLOCK_US
    offsets = [0]
    for k in range(1, n_y // 2 + 1):
        offsets += [-k, k] if 2 * k < n_y else [-k]
    add(("blend",), [], 0.3, rank=-3)
    for j in offsets:
        if j == 0:
            continue
        link = "y+" if j < 0 else "y-"
        sign = 1 if j > 0 else -1
        add(("wy", j), [("wy", j - sign)] if abs(j) > 1 else [("blend",)], w_cost, link)
    for slot, j in enumerate(offsets):
        source = ("wy", j) if j else ("blend",)
        cost = w_cost * (1 - LAST / 768 if abs(j) == 1 else 1)
        up = n_z // 2 - (slot % 2)
        for k in range(1, n_z // 2 + 1):
            for way, most in ((1, up), (-1, n_z - 1 - up)):
                if k <= most:
                    link = "z+" if way > 0 else "z-"
                    add(("wz", slot, way * k), [("wz", slot, way * (k - 1))] if k > 1 else [source], cost, link)
    add(("local",), [], 0.5, rank=-2)
    for h in range(heads):
        for i in range(2):
            add(("x", h, i), [], kv_cost / 2, "x")
    add(("xq",), [], kv_cost, "x")
    streams = [(h, own) for h in range(heads) for own in (1, 0)]
    hops = {1: (n_y // 2, n_y - 1 - n_y // 2), 0: (n_y - 1 - n_y // 2, n_y // 2)}
    for i, (h, own) in enumerate(streams):
        source = [("local",)] if own else [("x", h, 0), ("x", h, 1)]
        for k in range(1, n_y // 2 + 1):
            for way, most in zip((1, -1), hops[own]):
                if k <= most:
                    deps = [("kv", h, own, way * (k - 1))] if k > 1 else list(source)
                    if k == 1 and i >= WINDOW:
                        before = streams[i - WINDOW]
                        deps.append(("kv", *before, way * (hops[before[1]][way < 0] - 1)))
                    add(("kv", h, own, way * k), deps, kv_cost, "y+" if way > 0 else "y-")
    if LAST:
        gathered = [n.name for n in nodes if n.name[:2] == ("wz", 0)]
        for j in (-1, 1):
            late = [("kv", h, own, -j * hops[own][j > 0]) for h, own in streams]
            add(("yl", j), gathered + late, 13.0 * LAST / 768, "y+" if j < 0 else "y-")
    add(("mask",), [], 1.0, rank=-1)
    for h in range(heads):
        held = [("mask",), ("local",), ("x", h, 0), ("x", h, 1), ("xq",)]
        rest = [n.name for n in nodes if n.name[:2] == ("kv", h) and 2 * abs(n.name[3]) == n_y]
        held += [n.name for n in nodes if n.name[:2] == ("kv", h) and 2 * abs(n.name[3]) < n_y]
        for half in range(2):
            add(("near", h, half), held, 0.45)
            add(("far", h, half), [("near", h, half)] + rest, 0.15, rank=-5)
            add(("a", h, half), [("far", h, half)], 0.7, "x")
    ready = [("a", h, half) for h in range(heads) for half in range(2)]
    for slot, j in enumerate(offsets):
        shards = [n.name for n in nodes if n.name[0] == "wz" and n.name[1] == slot]
        source = [("wy", j)] if j else [("blend",)]
        if LAST and abs(j) == 1:
            source.append(("yl", j))
        add(("pre", slot), ready[:-2] + shards + source, 0.35, rank=slot + 30)
        add(("proj", slot), ready[-2:] + [("pre", slot)], 0.2, rank=slot)
        add(("c", slot), [("proj", slot)], 0.3, "core")
        add(("add", slot), [("c", slot)], 0.1, rank=slot - 20)
        for r in range(3):
            add(("e", slot, r), [("add", slot)], 1.0, "x%d" % r)
        add(("sum", slot), [("e", slot, r) for r in range(3)], 0.1, rank=slot + 20)
    add(("last",), [("sum", slot) for slot in range(n_y)], 0.5, rank=100)
    return nodes, offsets


def kernel(
    n_y, n_z, order, ids, offsets,
    q_hbm, k_hbm, v_hbm, seg_hbm, blend_ref, first_hbm, second_hbm, out_ref,
    seg_ref, w_in, kvbuf, qbuf, bias, stats, wbuf, attbuf, acc, p_all, c_recv, s_send, s_keep, e_recv, out_t,
    local_sem, send_sem, recv_sem,
):
    z = lax.axis_index("dp")
    f = lax.axis_index("fsdp")
    t = lax.axis_index("tensor")
    y, x = f // 2, f % 2
    x_hi, core = t // 2, t % 2
    rows = q_hbm.shape[1]
    half_width = q_hbm.shape[2] // 2
    heads = half_width // HEAD_DIM
    piece, split = w_in.shape[1], w_in.shape[2] - LAST
    x_other = f + 1 - 2 * x
    t_core = t + 1 - 2 * core
    t_hi = t + 2 - 4 * x_hi

    ys = [(y + d) % n_y for d in range(n_y)]
    zs = [(z + d) % n_z for d in range(n_z)]

    def y_at(d):
        return ys[d % n_y]

    def z_at(d):
        return zs[d % n_z]

    def to(dp=None, fsdp=None, tensor=None):
        return (z if dp is None else dp, f if fsdp is None else fsdp, t if tensor is None else tensor)

    partners = [
        to(fsdp=x_other),
        to(tensor=t_core),
        to(tensor=t_hi),
        to(fsdp=x_other, tensor=t_hi),
        to(fsdp=y_at(1) * 2 + x),
        to(fsdp=y_at(-1) * 2 + x),
        to(dp=z_at(1)),
        to(dp=z_at(-1)),
    ]

    mine = pl.ds(pl.multiple_of(x * half_width, HEAD_DIM), half_width)
    theirs = pl.ds(pl.multiple_of((1 - x) * half_width, HEAD_DIM), half_width)

    def token_rows(y_index, x_index):
        return pl.ds(pl.multiple_of((y_index * 2 + x_index) * rows, rows), rows)

    def head_of(x_index, h):
        return pl.ds(pl.multiple_of((x_index * heads + h) * HEAD_DIM, HEAD_DIM), HEAD_DIM)

    def q_rows(x_index):
        return pl.ds(pl.multiple_of(x_index * rows, rows), rows)

    weights = [
        pltpu.make_async_copy(first_hbm, w_in.at[0], local_sem.at[1 + 2 * heads]),
        pltpu.make_async_copy(second_hbm, w_in.at[1], local_sem.at[2 + 2 * heads]),
    ]
    ids_copy = pltpu.make_async_copy(seg_hbm, seg_ref, local_sem.at[3 + 2 * heads])
    locals_ = [pltpu.make_async_copy(q_hbm.at[0, :, mine], qbuf.at[q_rows(x)], local_sem.at[0])]
    for h in range(heads):
        for i, source in enumerate((k_hbm, v_hbm)):
            locals_.append(
                pltpu.make_async_copy(
                    source.at[0, :, head_of(x, h)], kvbuf.at[h, i, token_rows(y, x)], local_sem.at[1 + 2 * h + i]
                )
            )
    for copy in weights + locals_ + [ids_copy]:
        copy.start()

    barrier = pltpu.get_barrier_semaphore()
    for partner in partners:
        pl.semaphore_signal(barrier, inc=1, device_id=partner, device_id_type=MESH)
    pl.semaphore_wait(barrier, len(partners))

    def copy_of(name, arriving):
        kind = name[0]
        if kind == "wy":
            j = name[1]
            sign = 1 if j > 0 else -1
            src = dst = wbuf.at[y_at(j if arriving else j - sign), z]
            who = to(fsdp=y_at(-sign) * 2 + x)
        elif kind == "wz":
            slot, k = name[1:]
            way = 1 if k > 0 else -1
            src = dst = wbuf.at[y_at(offsets[slot]), z_at(-k if arriving else -(k - way))]
            if abs(offsets[slot]) == 1 and LAST:
                src = dst = src.at[:, :split]
            who = to(dp=z_at(way))
        elif kind == "yl":
            j = name[1]
            src = dst = wbuf.at[y_at(j if arriving else 0), :, :, split:]
            who = to(fsdp=y_at(-j) * 2 + x)
        elif kind == "xq":
            dst = qbuf.at[q_rows(1 - x if arriving else x)]
            src = dst if arriving else q_hbm.at[0, :, theirs]
            who = to(fsdp=x_other)
        elif kind == "x":
            h, i = name[1:]
            dst = kvbuf.at[h, i, token_rows(y, 1 - x if arriving else x)]
            src = dst if arriving else (k_hbm, v_hbm)[i].at[0, :, head_of(1 - x, h)]
            who = to(fsdp=x_other)
        elif kind == "kv":
            h, own, k = name[1:]
            way = 1 if k > 0 else -1
            part_x = x if own else 1 - x
            src = dst = kvbuf.at[h, :, token_rows(y_at(-k if arriving else -(k - way)), part_x)]
            who = to(fsdp=y_at(way) * 2 + x)
        elif kind == "a":
            h, half = name[1:]
            src = dst = attbuf.at[((1 - x) if arriving else x) * heads + h, half * rows : (half + 1) * rows]
            who = to(fsdp=x_other)
        elif kind == "c":
            slot = name[1]
            dst = c_recv.at[slot]
            src = dst if arriving else p_all.at[slot, :, 1 - core]
            who = to(tensor=t_core)
        else:
            slot, r = name[1:]
            dst = e_recv.at[r, slot]
            src = dst if arriving else s_send.at[r, slot]
            who = partners[(2, 3, 0)[r]]
        i = ids[name]
        return pltpu.make_async_remote_copy(
            src_ref=src, dst_ref=dst, send_sem=send_sem.at[i], recv_sem=recv_sem.at[i],
            device_id=who, device_id_type=MESH,
        )

    def blend():
        for copy in weights:
            copy.wait()
        coef = blend_ref[0]
        mixed = (1.0 - coef) * w_in[0].astype(jnp.float32) + coef * w_in[1].astype(jnp.float32)
        wbuf[y, z] = mixed.astype(jnp.bfloat16)

    def mask():
        ids_copy.wait()
        count = 2 * rows
        row = seg_ref[:, pl.ds(pl.multiple_of(y * count, count), count)].astype(jnp.float32)
        on = lax.broadcasted_iota(jnp.int32, (count, count), 0) == lax.broadcasted_iota(jnp.int32, (count, count), 1)
        column = jnp.sum(jnp.where(on, jnp.broadcast_to(row, (count, count)), 0.0), axis=1, keepdims=True)
        keys = seg_ref[...].astype(jnp.float32)
        bias[...] = jnp.where(column == keys, jnp.float32(0.0), jnp.float32(-1e30))

    def scores_of(h, half, j):
        at, cols = slice(half * rows, (half + 1) * rows), slice(h * HEAD_DIM, (h + 1) * HEAD_DIM)
        keys = pl.ds(pl.multiple_of(y_at(j) * 2 * rows, 2 * rows), 2 * rows)
        scores = lax.dot_general(qbuf[at, cols], kvbuf[h, 0, keys], NT, preferred_element_type=jnp.float32)
        return scores * HEAD_DIM ** (-0.5) + bias[at, keys], keys

    def near(h, half):
        blocks = [scores_of(h, half, j) for j in range(1 - n_y // 2, n_y // 2)]
        top = jnp.max(functools.reduce(jnp.maximum, [scores for scores, _ in blocks]), axis=1, keepdims=True)
        expos = [jnp.exp(scores - top) for scores, _ in blocks]
        total = jnp.sum(functools.reduce(jnp.add, expos), axis=1, keepdims=True)
        result = jnp.zeros((rows, HEAD_DIM), jnp.float32)
        for expo, (_, keys) in zip(expos, blocks):
            result += jnp.dot(expo.astype(jnp.bfloat16), kvbuf[h, 1, keys], preferred_element_type=jnp.float32)
        stats[h, half, 0] = jnp.broadcast_to(top, (rows, HEAD_DIM))
        stats[h, half, 1] = jnp.broadcast_to(total, (rows, HEAD_DIM))
        stats[h, half, 2] = result

    def far(h, half):
        scores, keys = scores_of(h, half, n_y // 2)
        before = stats[h, half, 0][:, :1]
        top = jnp.maximum(before, jnp.max(scores, axis=1, keepdims=True))
        expo, shrink = jnp.exp(scores - top), jnp.exp(before - top)
        total = stats[h, half, 1][:, :1] * shrink + jnp.sum(expo, axis=1, keepdims=True)
        result = jnp.dot(expo.astype(jnp.bfloat16), kvbuf[h, 1, keys], preferred_element_type=jnp.float32)
        result = (stats[h, half, 2] * shrink + result) / total
        attbuf[x * heads + h, half * rows : (half + 1) * rows, :] = result.astype(jnp.bfloat16)

    def product(slot, spans):
        at = y_at(offsets[slot])
        weight = jnp.concatenate(
            [wbuf[at, :, :, a * HEAD_DIM : b * HEAD_DIM].reshape(n_z * piece, (b - a) * HEAD_DIM) for a, b in spans], axis=1
        )
        attended = jnp.concatenate([attbuf[i] for a, b in spans for i in range(a, b)], axis=1)
        return lax.dot_general(weight, attended, NT, preferred_element_type=jnp.float32)

    def pre(slot):
        acc[slot] = product(slot, [(0, heads - 1), (heads, 2 * heads - 1)])

    def proj(slot):
        part = acc[slot] + product(slot, [(heads - 1, heads), (2 * heads - 1, 2 * heads)])
        p_all[slot] = part.astype(jnp.bfloat16).reshape(p_all.shape[1:])

    def add(slot):
        for away in range(2):
            hi = (1 - x_hi) if away else x_hi
            both = (p_all[slot, hi, core].astype(jnp.float32) + c_recv[slot, hi].astype(jnp.float32)).astype(jnp.bfloat16)
            first, second = both[:, :rows], both[:, rows:]
            keep = jnp.where(x == 0, first, second)
            move = jnp.where(x == 0, second, first)
            if away:
                s_send[0, slot] = keep
                s_send[1, slot] = move
            else:
                s_keep[slot] = keep
                s_send[2, slot] = move

    def total(slot):
        at = y_at(offsets[slot])
        per = n_z // 4
        own = s_keep[slot].astype(jnp.float32) + e_recv[0, slot].astype(jnp.float32)
        other = e_recv[1, slot].astype(jnp.float32) + e_recv[2, slot].astype(jnp.float32)
        for i in range(per):
            part = slice(i * piece, (i + 1) * piece)
            out_t[i, at, x] = own[part].astype(jnp.bfloat16)
            out_t[i, at, 1 - x] = other[part].astype(jnp.bfloat16)

    def last():
        eye = lax.broadcasted_iota(jnp.int32, (rows, rows), 0) == lax.broadcasted_iota(jnp.int32, (rows, rows), 1)
        eye = jnp.where(eye, 1.0, 0.0).astype(jnp.bfloat16)
        flat = out_t[...].reshape(out_ref.shape[2], rows)
        out_ref[0] = lax.dot_general(eye, flat, NT, preferred_element_type=jnp.float32).astype(jnp.bfloat16)

    def local():
        for copy in locals_:
            copy.wait()

    work = {
        "blend": blend, "mask": mask, "near": near, "far": far, "pre": pre, "proj": proj, "add": add, "sum": total, "last": last, "local": local,
    }
    for verb, name in order:
        if verb == "start":
            copy_of(name, False).start()
        elif verb == "wait":
            copy_of(name, True).wait_recv()
        elif verb == "sent":
            copy_of(name, False).wait_send()
        else:
            work[name[0]](*name[1:])


def per_device(n_y, n_z, query, key_in, value, segment_ids, blend, w_first, w_second):
    rows, width = query.shape[1], query.shape[2]
    heads = width // HEAD_DIM // 2
    half = width // 2
    patches = segment_ids.shape[1]
    piece = w_first.shape[0]
    nodes, offsets = plan(n_y, n_z, heads)
    order = order_of(nodes)
    ids = {}
    for node in nodes:
        if node.link is not None:
            ids[node.name] = len(ids)
    bf16, f32 = jnp.bfloat16, jnp.float32
    group = n_z // 4 * piece
    any_, vmem = pl.BlockSpec(memory_space=pl.ANY), pl.BlockSpec(memory_space=pltpu.VMEM)
    out_cols = 2 * n_y * group
    return pl.pallas_call(
        functools.partial(kernel, n_y, n_z, order, ids, offsets),
        out_shape=jax.ShapeDtypeStruct((1, rows, out_cols), bf16),
        in_specs=[any_, any_, any_, any_, pl.BlockSpec(memory_space=pltpu.SMEM), any_, any_],
        out_specs=vmem,
        scratch_shapes=[
            pltpu.VMEM((1, patches), jnp.int32),
            pltpu.VMEM((2, piece, width), bf16),
            pltpu.VMEM((heads, 2, patches, HEAD_DIM), bf16),
            pltpu.VMEM((2 * rows, half), bf16),
            pltpu.VMEM((2 * rows, patches), f32),
            pltpu.VMEM((heads, 2, 3, rows, HEAD_DIM), f32),
            pltpu.VMEM((n_y, n_z, piece, width), bf16),
            pltpu.VMEM((2 * heads, 2 * rows, HEAD_DIM), bf16),
            pltpu.VMEM((n_y, n_z * piece, 2 * rows), f32),
            pltpu.VMEM((n_y, 2, 2, group, 2 * rows), bf16),
            pltpu.VMEM((n_y, 2, group, 2 * rows), bf16),
            pltpu.VMEM((3, n_y, group, rows), bf16),
            pltpu.VMEM((n_y, group, rows), bf16),
            pltpu.VMEM((3, n_y, group, rows), bf16),
            pltpu.VMEM((n_z // 4, n_y, 2, piece, rows), bf16),
            pltpu.SemaphoreType.DMA((4 + 2 * heads,)),
            pltpu.SemaphoreType.DMA((len(ids),)),
            pltpu.SemaphoreType.DMA((len(ids),)),
        ],
        compiler_params=pltpu.CompilerParams(
            collective_id=0, has_side_effects=True, vmem_limit_bytes=62 * 1024 * 1024
        ),
    )(query, key_in, value, segment_ids, blend, w_first, w_second)


def solution(mesh):
    in_specs = (
        P("dp", "fsdp", "tensor"),
        P("dp", "fsdp", "tensor"),
        P("dp", "fsdp", "tensor"),
        P("dp", None),
        P(),
        P(("dp", "fsdp"), "tensor"),
        P(("dp", "fsdp"), "tensor"),
    )
    out_specs = P("dp", "fsdp", "tensor")
    body = functools.partial(per_device, mesh.shape["fsdp"] // 2, mesh.shape["dp"])
    return jax.shard_map(body, mesh=mesh, in_specs=in_specs, out_specs=out_specs, check_vma=False)
```

```python
import functools
import heapq

import jax
import jax.numpy as jnp
from jax import lax
from jax.experimental import pallas as pl
from jax.experimental.pallas import tpu as pltpu
from jax.sharding import PartitionSpec as P

HEAD_DIM = 128
LAST = 256
IDLE = 4
WINDOW = 6
LATENCY, LATENCY_ELSE = {"y": 2.04, "z": 1.97}, 2.21
SHARD_US, BLOCK_US = 1.558, 1.346
MESH = pl.DeviceIdType.MESH
NT = (((1,), (1,)), ((), ()))


class Node:
    def __init__(self, name, deps, cost, link=None, rank=0):
        self.name, self.deps, self.cost, self.link, self.rank = name, list(deps), cost, link, rank


def order_of(nodes):
    by_name = {node.name: node for node in nodes}
    position = {node.name: i for i, node in enumerate(nodes)}
    feeds = {node.name: False for node in nodes}
    for node in nodes:
        if node.link is not None:
            for dep in node.deps:
                feeds[dep] = True
    done, started, waited = set(), set(), set()
    arrivals, free, order, now = [], {}, [], 0.0
    flying = []
    while len(done) < len(nodes):
        for node in nodes:
            if node.link is not None and node.name not in started and all(d in done for d in node.deps):
                for d in node.deps:
                    if by_name[d].link is not None and d not in waited:
                        waited.add(d)
                        order.append(("wait", d))
                started.add(node.name)
                order.append(("start", node.name))
                begin = max(now, free.get(node.link, 0.0))
                free[node.link] = begin + node.cost
                landing = begin + node.cost + LATENCY.get(node.link[0], LATENCY_ELSE)
                heapq.heappush(arrivals, (landing, position[node.name], node.name))
                flying.append((landing, node.name))
        if arrivals and arrivals[0][0] <= now:
            name = heapq.heappop(arrivals)[2]
            done.add(name)
            if feeds[name] and name not in waited:
                waited.add(name)
                order.append(("wait", name))
            continue
        ready = [n for n in nodes if n.link is None and n.name not in done and all(d in done for d in n.deps)]
        if ready:
            node = min(ready, key=lambda n: (n.rank, position[n.name]))
            for d in node.deps:
                if by_name[d].link is not None and d not in waited:
                    waited.add(d)
                    order.append(("wait", d))
            order.append(("compute", node.name))
            now += node.cost
            done.add(node.name)
            continue
        for item in sorted(flying)[:IDLE]:
            if item[0] + 1.0 < now:
                flying.remove(item)
                order.append(("sent", item[1]))
        now = max(now, arrivals[0][0])
    return order + [("sent", name) for _, name in sorted(flying)]


def plan(n_y, n_z, heads):
    nodes = []

    def add(name, deps, cost, link=None, rank=0):
        nodes.append(Node(name, deps, cost, link, rank))
        return name

    w_cost, kv_cost = SHARD_US, BLOCK_US
    offsets = [0]
    for k in range(1, n_y // 2 + 1):
        offsets += [-k, k] if 2 * k < n_y else [-k]
    add(("blend",), [], 0.3, rank=-3)
    for j in offsets:
        if j == 0:
            continue
        link = "y+" if j < 0 else "y-"
        sign = 1 if j > 0 else -1
        add(("wy", j), [("wy", j - sign)] if abs(j) > 1 else [("blend",)], w_cost, link)
    for slot, j in enumerate(offsets):
        source = ("wy", j) if j else ("blend",)
        cost = w_cost * (1 - LAST / 768 if abs(j) == 1 else 1)
        up = n_z // 2 - (slot % 2)
        for k in range(1, n_z // 2 + 1):
            for way, most in ((1, up), (-1, n_z - 1 - up)):
                if k <= most:
                    link = "z+" if way > 0 else "z-"
                    add(("wz", slot, way * k), [("wz", slot, way * (k - 1))] if k > 1 else [source], cost, link)
    add(("local",), [], 0.5, rank=-2)
    for h in range(heads):
        for i in range(2):
            add(("x", h, i), [], kv_cost / 2, "x")
    add(("xq",), [], kv_cost, "x")
    streams = [(h, own) for h in range(heads) for own in (1, 0)]
    hops = {1: (n_y // 2, n_y - 1 - n_y // 2), 0: (n_y - 1 - n_y // 2, n_y // 2)}
    for i, (h, own) in enumerate(streams):
        source = [("local",)] if own else [("x", h, 0), ("x", h, 1)]
        for k in range(1, n_y // 2 + 1):
            for way, most in zip((1, -1), hops[own]):
                if k <= most:
                    deps = [("kv", h, own, way * (k - 1))] if k > 1 else list(source)
                    if k == 1 and i >= WINDOW:
                        before = streams[i - WINDOW]
                        deps.append(("kv", *before, way * (hops[before[1]][way < 0] - 1)))
                    add(("kv", h, own, way * k), deps, kv_cost, "y+" if way > 0 else "y-")
    if LAST:
        gathered = [n.name for n in nodes if n.name[:2] == ("wz", 0)]
        for j in (-1, 1):
            late = [("kv", h, own, -j * hops[own][j > 0]) for h, own in streams]
            add(("yl", j), gathered + late, 13.0 * LAST / 768, "y+" if j < 0 else "y-")
    add(("mask",), [], 1.0, rank=-1)
    for h in range(heads):
        held = [("mask",), ("local",), ("x", h, 0), ("x", h, 1), ("xq",)]
        rest = [n.name for n in nodes if n.name[:2] == ("kv", h) and 2 * abs(n.name[3]) == n_y]
        held += [n.name for n in nodes if n.name[:2] == ("kv", h) and 2 * abs(n.name[3]) < n_y]
        for half in range(2):
            add(("near", h, half), held, 0.56)
            add(("far", h, half), [("near", h, half)] + rest, 0.15, rank=-5)
            add(("a", h, half), [("far", h, half)], 0.7, "x")
    ready = [("a", h, half) for h in range(heads) for half in range(2)]
    for slot, j in enumerate(offsets):
        shards = [n.name for n in nodes if n.name[0] == "wz" and n.name[1] == slot]
        source = [("wy", j)] if j else [("blend",)]
        if LAST and abs(j) == 1:
            source.append(("yl", j))
        add(("pre", slot), ready[:-2] + shards + source, 0.35, rank=slot + 30)
        add(("proj", slot), ready[-2:] + [("pre", slot)], 0.2, rank=slot)
        add(("c", slot), [("proj", slot)], 0.3, "core")
        add(("add", slot), [("c", slot)], 0.1, rank=slot - 20)
        for r in range(3):
            add(("e", slot, r), [("add", slot)], 1.0, "x%d" % r)
        add(("sum", slot), [("e", slot, r) for r in range(3)], 0.1, rank=slot + 20)
    add(("last",), [("sum", slot) for slot in range(n_y)], 0.5, rank=100)
    return nodes, offsets


def kernel(
    n_y, n_z, order, ids, offsets,
    q_hbm, k_hbm, v_hbm, seg_hbm, blend_ref, first_hbm, second_hbm, out_ref,
    seg_ref, w_in, kvbuf, qbuf, bias, stats, wbuf, attbuf, acc, p_all, c_recv, s_send, s_keep, e_recv, out_t,
    local_sem, send_sem, recv_sem,
):
    z = lax.axis_index("dp")
    f = lax.axis_index("fsdp")
    t = lax.axis_index("tensor")
    y, x = f // 2, f % 2
    x_hi, core = t // 2, t % 2
    rows = q_hbm.shape[1]
    half_width = q_hbm.shape[2] // 2
    heads = half_width // HEAD_DIM
    piece, split = w_in.shape[1], w_in.shape[2] - LAST
    x_other = f + 1 - 2 * x
    t_core = t + 1 - 2 * core
    t_hi = t + 2 - 4 * x_hi

    ys = [(y + d) % n_y for d in range(n_y)]
    zs = [(z + d) % n_z for d in range(n_z)]

    def y_at(d):
        return ys[d % n_y]

    def z_at(d):
        return zs[d % n_z]

    def to(dp=None, fsdp=None, tensor=None):
        return (z if dp is None else dp, f if fsdp is None else fsdp, t if tensor is None else tensor)

    partners = [
        to(fsdp=x_other),
        to(tensor=t_core),
        to(tensor=t_hi),
        to(fsdp=x_other, tensor=t_hi),
        to(fsdp=y_at(1) * 2 + x),
        to(fsdp=y_at(-1) * 2 + x),
        to(dp=z_at(1)),
        to(dp=z_at(-1)),
    ]

    mine = pl.ds(pl.multiple_of(x * half_width, HEAD_DIM), half_width)
    theirs = pl.ds(pl.multiple_of((1 - x) * half_width, HEAD_DIM), half_width)

    def token_rows(y_index, x_index):
        return pl.ds(pl.multiple_of((y_index * 2 + x_index) * rows, rows), rows)

    def head_of(x_index, h):
        return pl.ds(pl.multiple_of((x_index * heads + h) * HEAD_DIM, HEAD_DIM), HEAD_DIM)

    def q_rows(x_index):
        return pl.ds(pl.multiple_of(x_index * rows, rows), rows)

    weights = [
        pltpu.make_async_copy(first_hbm, w_in.at[0], local_sem.at[1 + 2 * heads]),
        pltpu.make_async_copy(second_hbm, w_in.at[1], local_sem.at[2 + 2 * heads]),
    ]
    ids_copy = pltpu.make_async_copy(seg_hbm, seg_ref, local_sem.at[3 + 2 * heads])
    locals_ = [pltpu.make_async_copy(q_hbm.at[0, :, mine], qbuf.at[q_rows(x)], local_sem.at[0])]
    for h in range(heads):
        for i, source in enumerate((k_hbm, v_hbm)):
            locals_.append(
                pltpu.make_async_copy(
                    source.at[0, :, head_of(x, h)], kvbuf.at[h, i, token_rows(y, x)], local_sem.at[1 + 2 * h + i]
                )
            )
    for copy in weights + locals_ + [ids_copy]:
        copy.start()

    barrier = pltpu.get_barrier_semaphore()
    for partner in partners:
        pl.semaphore_signal(barrier, inc=1, device_id=partner, device_id_type=MESH)
    pl.semaphore_wait(barrier, len(partners))

    def copy_of(name, arriving):
        kind = name[0]
        if kind == "wy":
            j = name[1]
            sign = 1 if j > 0 else -1
            src = dst = wbuf.at[y_at(j if arriving else j - sign), z]
            who = to(fsdp=y_at(-sign) * 2 + x)
        elif kind == "wz":
            slot, k = name[1:]
            way = 1 if k > 0 else -1
            src = dst = wbuf.at[y_at(offsets[slot]), z_at(-k if arriving else -(k - way))]
            if abs(offsets[slot]) == 1 and LAST:
                src = dst = src.at[:, :split]
            who = to(dp=z_at(way))
        elif kind == "yl":
            j = name[1]
            src = dst = wbuf.at[y_at(j if arriving else 0), :, :, split:]
            who = to(fsdp=y_at(-j) * 2 + x)
        elif kind == "xq":
            dst = qbuf.at[q_rows(1 - x if arriving else x)]
            src = dst if arriving else q_hbm.at[0, :, theirs]
            who = to(fsdp=x_other)
        elif kind == "x":
            h, i = name[1:]
            dst = kvbuf.at[h, i, token_rows(y, 1 - x if arriving else x)]
            src = dst if arriving else (k_hbm, v_hbm)[i].at[0, :, head_of(1 - x, h)]
            who = to(fsdp=x_other)
        elif kind == "kv":
            h, own, k = name[1:]
            way = 1 if k > 0 else -1
            part_x = x if own else 1 - x
            src = dst = kvbuf.at[h, :, token_rows(y_at(-k if arriving else -(k - way)), part_x)]
            who = to(fsdp=y_at(way) * 2 + x)
        elif kind == "a":
            h, half = name[1:]
            src = dst = attbuf.at[((1 - x) if arriving else x) * heads + h, half * rows : (half + 1) * rows]
            who = to(fsdp=x_other)
        elif kind == "c":
            slot = name[1]
            dst = c_recv.at[slot]
            src = dst if arriving else p_all.at[slot, :, 1 - core]
            who = to(tensor=t_core)
        else:
            slot, r = name[1:]
            dst = e_recv.at[r, slot]
            src = dst if arriving else s_send.at[r, slot]
            who = partners[(2, 3, 0)[r]]
        i = ids[name]
        return pltpu.make_async_remote_copy(
            src_ref=src, dst_ref=dst, send_sem=send_sem.at[i], recv_sem=recv_sem.at[i],
            device_id=who, device_id_type=MESH,
        )

    def blend():
        for copy in weights:
            copy.wait()
        coef = blend_ref[0]
        mixed = (1.0 - coef) * w_in[0].astype(jnp.float32) + coef * w_in[1].astype(jnp.float32)
        wbuf[y, z] = mixed.astype(jnp.bfloat16)

    def mask():
        ids_copy.wait()
        count = 2 * rows
        row = seg_ref[:, pl.ds(pl.multiple_of(y * count, count), count)].astype(jnp.float32)
        on = lax.broadcasted_iota(jnp.int32, (count, count), 0) == lax.broadcasted_iota(jnp.int32, (count, count), 1)
        column = jnp.sum(jnp.where(on, jnp.broadcast_to(row, (count, count)), 0.0), axis=1, keepdims=True)
        keys = seg_ref[...].astype(jnp.float32)
        bias[...] = jnp.where(column == keys, jnp.float32(0.0), jnp.float32(-1e30))

    def scores_of(h, half, j):
        at, cols = slice(half * rows, (half + 1) * rows), slice(h * HEAD_DIM, (h + 1) * HEAD_DIM)
        keys = pl.ds(pl.multiple_of(y_at(j) * 2 * rows, 2 * rows), 2 * rows)
        scores = lax.dot_general(qbuf[at, cols], kvbuf[h, 0, keys], NT, preferred_element_type=jnp.float32)
        return scores * HEAD_DIM ** (-0.5) + bias[at, keys], keys

    def near(h, half):
        blocks = [scores_of(h, half, j) for j in range(1 - n_y // 2, n_y // 2)]
        top = jnp.max(functools.reduce(jnp.maximum, [scores for scores, _ in blocks]), axis=1, keepdims=True)
        expos = [jnp.exp(scores - top) for scores, _ in blocks]
        total = jnp.sum(functools.reduce(jnp.add, expos), axis=1, keepdims=True)
        result = jnp.zeros((rows, HEAD_DIM), jnp.float32)
        for expo, (_, keys) in zip(expos, blocks):
            result += jnp.dot(expo.astype(jnp.bfloat16), kvbuf[h, 1, keys], preferred_element_type=jnp.float32)
        stats[h, half, 0] = jnp.broadcast_to(top, (rows, HEAD_DIM))
        stats[h, half, 1] = jnp.broadcast_to(total, (rows, HEAD_DIM))
        stats[h, half, 2] = result

    def far(h, half):
        scores, keys = scores_of(h, half, n_y // 2)
        before = stats[h, half, 0][:, :1]
        top = jnp.maximum(before, jnp.max(scores, axis=1, keepdims=True))
        expo, shrink = jnp.exp(scores - top), jnp.exp(before - top)
        total = stats[h, half, 1][:, :1] * shrink + jnp.sum(expo, axis=1, keepdims=True)
        result = jnp.dot(expo.astype(jnp.bfloat16), kvbuf[h, 1, keys], preferred_element_type=jnp.float32)
        result = (stats[h, half, 2] * shrink + result) / total
        attbuf[x * heads + h, half * rows : (half + 1) * rows, :] = result.astype(jnp.bfloat16)

    def product(slot, spans):
        at = y_at(offsets[slot])
        weight = jnp.concatenate(
            [wbuf[at, :, :, a * HEAD_DIM : b * HEAD_DIM].reshape(n_z * piece, (b - a) * HEAD_DIM) for a, b in spans], axis=1
        )
        attended = jnp.concatenate([attbuf[i] for a, b in spans for i in range(a, b)], axis=1)
        return lax.dot_general(weight, attended, NT, preferred_element_type=jnp.float32)

    def pre(slot):
        acc[slot] = product(slot, [(0, heads - 1), (heads, 2 * heads - 1)])

    def proj(slot):
        part = acc[slot] + product(slot, [(heads - 1, heads), (2 * heads - 1, 2 * heads)])
        p_all[slot] = part.astype(jnp.bfloat16).reshape(p_all.shape[1:])

    def add(slot):
        for away in range(2):
            hi = (1 - x_hi) if away else x_hi
            both = (p_all[slot, hi, core].astype(jnp.float32) + c_recv[slot, hi].astype(jnp.float32)).astype(jnp.bfloat16)
            first, second = both[:, :rows], both[:, rows:]
            keep = jnp.where(x == 0, first, second)
            move = jnp.where(x == 0, second, first)
            if away:
                s_send[0, slot] = keep
                s_send[1, slot] = move
            else:
                s_keep[slot] = keep
                s_send[2, slot] = move

    def total(slot):
        at = y_at(offsets[slot])
        per = n_z // 4
        own = s_keep[slot].astype(jnp.float32) + e_recv[0, slot].astype(jnp.float32)
        other = e_recv[1, slot].astype(jnp.float32) + e_recv[2, slot].astype(jnp.float32)
        for i in range(per):
            part = slice(i * piece, (i + 1) * piece)
            out_t[i, at, x] = own[part].astype(jnp.bfloat16)
            out_t[i, at, 1 - x] = other[part].astype(jnp.bfloat16)

    def last():
        eye = lax.broadcasted_iota(jnp.int32, (rows, rows), 0) == lax.broadcasted_iota(jnp.int32, (rows, rows), 1)
        eye = jnp.where(eye, 1.0, 0.0).astype(jnp.bfloat16)
        flat = out_t[...].reshape(out_ref.shape[2], rows)
        out_ref[0] = lax.dot_general(eye, flat, NT, preferred_element_type=jnp.float32).astype(jnp.bfloat16)

    def local():
        for copy in locals_:
            copy.wait()

    work = {
        "blend": blend, "mask": mask, "near": near, "far": far, "pre": pre, "proj": proj, "add": add, "sum": total, "last": last, "local": local,
    }
    for verb, name in order:
        if verb == "start":
            copy_of(name, False).start()
        elif verb == "wait":
            copy_of(name, True).wait_recv()
        elif verb == "sent":
            copy_of(name, False).wait_send()
        else:
            work[name[0]](*name[1:])


def per_device(n_y, n_z, query, key_in, value, segment_ids, blend, w_first, w_second):
    rows, width = query.shape[1], query.shape[2]
    heads = width // HEAD_DIM // 2
    half = width // 2
    patches = segment_ids.shape[1]
    piece = w_first.shape[0]
    nodes, offsets = plan(n_y, n_z, heads)
    order = order_of(nodes)
    ids = {}
    for node in nodes:
        if node.link is not None:
            ids[node.name] = len(ids)
    bf16, f32 = jnp.bfloat16, jnp.float32
    group = n_z // 4 * piece
    any_, vmem = pl.BlockSpec(memory_space=pl.ANY), pl.BlockSpec(memory_space=pltpu.VMEM)
    out_cols = 2 * n_y * group
    return pl.pallas_call(
        functools.partial(kernel, n_y, n_z, order, ids, offsets),
        out_shape=jax.ShapeDtypeStruct((1, rows, out_cols), bf16),
        in_specs=[any_, any_, any_, any_, pl.BlockSpec(memory_space=pltpu.SMEM), any_, any_],
        out_specs=vmem,
        scratch_shapes=[
            pltpu.VMEM((1, patches), jnp.int32),
            pltpu.VMEM((2, piece, width), bf16),
            pltpu.VMEM((heads, 2, patches, HEAD_DIM), bf16),
            pltpu.VMEM((2 * rows, half), bf16),
            pltpu.VMEM((2 * rows, patches), f32),
            pltpu.VMEM((heads, 2, 3, rows, HEAD_DIM), f32),
            pltpu.VMEM((n_y, n_z, piece, width), bf16),
            pltpu.VMEM((2 * heads, 2 * rows, HEAD_DIM), bf16),
            pltpu.VMEM((n_y, n_z * piece, 2 * rows), f32),
            pltpu.VMEM((n_y, 2, 2, group, 2 * rows), bf16),
            pltpu.VMEM((n_y, 2, group, 2 * rows), bf16),
            pltpu.VMEM((3, n_y, group, rows), bf16),
            pltpu.VMEM((n_y, group, rows), bf16),
            pltpu.VMEM((3, n_y, group, rows), bf16),
            pltpu.VMEM((n_z // 4, n_y, 2, piece, rows), bf16),
            pltpu.SemaphoreType.DMA((4 + 2 * heads,)),
            pltpu.SemaphoreType.DMA((len(ids),)),
            pltpu.SemaphoreType.DMA((len(ids),)),
        ],
        compiler_params=pltpu.CompilerParams(
            collective_id=0, has_side_effects=True, vmem_limit_bytes=62 * 1024 * 1024
        ),
    )(query, key_in, value, segment_ids, blend, w_first, w_second)


def solution(mesh):
    in_specs = (
        P("dp", "fsdp", "tensor"),
        P("dp", "fsdp", "tensor"),
        P("dp", "fsdp", "tensor"),
        P("dp", None),
        P(),
        P(("dp", "fsdp"), "tensor"),
        P(("dp", "fsdp"), "tensor"),
    )
    out_specs = P("dp", "fsdp", "tensor")
    body = functools.partial(per_device, mesh.shape["fsdp"] // 2, mesh.shape["dp"])
    return jax.shard_map(body, mesh=mesh, in_specs=in_specs, out_specs=out_specs, check_vma=False)
```

```python
import functools
import heapq

import jax
import jax.numpy as jnp
from jax import lax
from jax.experimental import pallas as pl
from jax.experimental.pallas import tpu as pltpu
from jax.sharding import PartitionSpec as P

HEAD_DIM = 128
LAST = 256
IDLE = 4
WINDOW = 6
LATENCY, LATENCY_ELSE = {"y": 2.01, "z": 1.98}, 2.1
SHARD_US, BLOCK_US = 1.541, 1.353
MESH = pl.DeviceIdType.MESH
NT = (((1,), (1,)), ((), ()))


class Node:
    def __init__(self, name, deps, cost, link=None, rank=0):
        self.name, self.deps, self.cost, self.link, self.rank = name, list(deps), cost, link, rank


def order_of(nodes):
    by_name = {node.name: node for node in nodes}
    position = {node.name: i for i, node in enumerate(nodes)}
    feeds = {node.name: False for node in nodes}
    for node in nodes:
        if node.link is not None:
            for dep in node.deps:
                feeds[dep] = True
    done, started, waited = set(), set(), set()
    arrivals, free, order, now = [], {}, [], 0.0
    flying = []
    while len(done) < len(nodes):
        for node in nodes:
            if node.link is not None and node.name not in started and all(d in done for d in node.deps):
                for d in node.deps:
                    if by_name[d].link is not None and d not in waited:
                        waited.add(d)
                        order.append(("wait", d))
                started.add(node.name)
                order.append(("start", node.name))
                begin = max(now, free.get(node.link, 0.0))
                free[node.link] = begin + node.cost
                landing = begin + node.cost + LATENCY.get(node.link[0], LATENCY_ELSE)
                heapq.heappush(arrivals, (landing, position[node.name], node.name))
                flying.append((landing, node.name))
        if arrivals and arrivals[0][0] <= now:
            name = heapq.heappop(arrivals)[2]
            done.add(name)
            if feeds[name] and name not in waited:
                waited.add(name)
                order.append(("wait", name))
            continue
        ready = [n for n in nodes if n.link is None and n.name not in done and all(d in done for d in n.deps)]
        if ready:
            node = min(ready, key=lambda n: (n.rank, position[n.name]))
            for d in node.deps:
                if by_name[d].link is not None and d not in waited:
                    waited.add(d)
                    order.append(("wait", d))
            order.append(("compute", node.name))
            now += node.cost
            done.add(node.name)
            continue
        for item in sorted(flying)[:IDLE]:
            if item[0] + 1.0 < now:
                flying.remove(item)
                order.append(("sent", item[1]))
        now = max(now, arrivals[0][0])
    return order + [("sent", name) for _, name in sorted(flying)]


def plan(n_y, n_z, heads):
    nodes = []

    def add(name, deps, cost, link=None, rank=0):
        nodes.append(Node(name, deps, cost, link, rank))
        return name

    w_cost, kv_cost = SHARD_US, BLOCK_US
    offsets = [0]
    for k in range(1, n_y // 2 + 1):
        offsets += [-k, k] if 2 * k < n_y else [-k]
    add(("blend",), [], 0.3, rank=-3)
    for j in offsets:
        if j == 0:
            continue
        link = "y+" if j < 0 else "y-"
        sign = 1 if j > 0 else -1
        add(("wy", j), [("wy", j - sign)] if abs(j) > 1 else [("blend",)], w_cost, link)
    for slot, j in enumerate(offsets):
        source = ("wy", j) if j else ("blend",)
        cost = w_cost * (1 - LAST / 768 if abs(j) == 1 else 1)
        up = n_z // 2 - (slot % 2)
        for k in range(1, n_z // 2 + 1):
            for way, most in ((1, up), (-1, n_z - 1 - up)):
                if k <= most:
                    link = "z+" if way > 0 else "z-"
                    add(("wz", slot, way * k), [("wz", slot, way * (k - 1))] if k > 1 else [source], cost, link)
    add(("local",), [], 0.5, rank=-2)
    for h in range(heads):
        for i in range(2):
            add(("x", h, i), [], kv_cost / 2, "x")
    add(("xq",), [], kv_cost, "x")
    streams = [(h, own) for h in range(heads) for own in (1, 0)]
    hops = {1: (n_y // 2, n_y - 1 - n_y // 2), 0: (n_y - 1 - n_y // 2, n_y // 2)}
    for i, (h, own) in enumerate(streams):
        source = [("local",)] if own else [("x", h, 0), ("x", h, 1)]
        for k in range(1, n_y // 2 + 1):
            for way, most in zip((1, -1), hops[own]):
                if k <= most:
                    deps = [("kv", h, own, way * (k - 1))] if k > 1 else list(source)
                    if k == 1 and i >= WINDOW:
                        before = streams[i - WINDOW]
                        deps.append(("kv", *before, way * (hops[before[1]][way < 0] - 1)))
                    add(("kv", h, own, way * k), deps, kv_cost, "y+" if way > 0 else "y-")
    if LAST:
        gathered = [n.name for n in nodes if n.name[:2] == ("wz", 0)]
        for j in (-1, 1):
            late = [("kv", h, own, -j * hops[own][j > 0]) for h, own in streams]
            add(("yl", j), gathered + late, 13.0 * LAST / 768, "y+" if j < 0 else "y-")
    add(("mask",), [], 1.0, rank=-1)
    for h in range(heads):
        held = [("mask",), ("local",), ("x", h, 0), ("x", h, 1), ("xq",)]
        rest = [n.name for n in nodes if n.name[:2] == ("kv", h) and 2 * abs(n.name[3]) == n_y]
        held += [n.name for n in nodes if n.name[:2] == ("kv", h) and 2 * abs(n.name[3]) < n_y]
        for half in range(2):
            add(("near", h, half), held, 0.6)
            add(("far", h, half), [("near", h, half)] + rest, 0.15, rank=-5)
            add(("a", h, half), [("far", h, half)], 0.7, "x")
    ready = [("a", h, half) for h in range(heads) for half in range(2)]
    for slot, j in enumerate(offsets):
        shards = [n.name for n in nodes if n.name[0] == "wz" and n.name[1] == slot]
        source = [("wy", j)] if j else [("blend",)]
        if LAST and abs(j) == 1:
            source.append(("yl", j))
        add(("pre", slot), ready[:-2] + shards + source, 0.35, rank=slot + 30)
        add(("proj", slot), ready[-2:] + [("pre", slot)], 0.2, rank=slot)
        add(("c", slot), [("proj", slot)], 0.3, "core")
        add(("add", slot), [("c", slot)], 0.1, rank=slot - 20)
        for r in range(3):
            add(("e", slot, r), [("add", slot)], 1.0, "x%d" % r)
        add(("sum", slot), [("e", slot, r) for r in range(3)], 0.1, rank=slot + 20)
    add(("last",), [("sum", slot) for slot in range(n_y)], 0.5, rank=100)
    return nodes, offsets


def kernel(
    n_y, n_z, order, ids, offsets,
    q_hbm, k_hbm, v_hbm, seg_hbm, blend_ref, first_hbm, second_hbm, out_ref,
    seg_ref, w_in, kvbuf, qbuf, bias, stats, wbuf, attbuf, acc, p_all, c_recv, s_send, s_keep, e_recv, out_t,
    local_sem, send_sem, recv_sem,
):
    z = lax.axis_index("dp")
    f = lax.axis_index("fsdp")
    t = lax.axis_index("tensor")
    y, x = f // 2, f % 2
    x_hi, core = t // 2, t % 2
    rows = q_hbm.shape[1]
    half_width = q_hbm.shape[2] // 2
    heads = half_width // HEAD_DIM
    piece, split = w_in.shape[1], w_in.shape[2] - LAST
    x_other = f + 1 - 2 * x
    t_core = t + 1 - 2 * core
    t_hi = t + 2 - 4 * x_hi

    ys = [(y + d) % n_y for d in range(n_y)]
    zs = [(z + d) % n_z for d in range(n_z)]

    def y_at(d):
        return ys[d % n_y]

    def z_at(d):
        return zs[d % n_z]

    def to(dp=None, fsdp=None, tensor=None):
        return (z if dp is None else dp, f if fsdp is None else fsdp, t if tensor is None else tensor)

    partners = [
        to(fsdp=x_other),
        to(tensor=t_core),
        to(tensor=t_hi),
        to(fsdp=x_other, tensor=t_hi),
        to(fsdp=y_at(1) * 2 + x),
        to(fsdp=y_at(-1) * 2 + x),
        to(dp=z_at(1)),
        to(dp=z_at(-1)),
    ]

    mine = pl.ds(pl.multiple_of(x * half_width, HEAD_DIM), half_width)
    theirs = pl.ds(pl.multiple_of((1 - x) * half_width, HEAD_DIM), half_width)

    def token_rows(y_index, x_index):
        return pl.ds(pl.multiple_of((y_index * 2 + x_index) * rows, rows), rows)

    def head_of(x_index, h):
        return pl.ds(pl.multiple_of((x_index * heads + h) * HEAD_DIM, HEAD_DIM), HEAD_DIM)

    def q_rows(x_index):
        return pl.ds(pl.multiple_of(x_index * rows, rows), rows)

    weights = [
        pltpu.make_async_copy(first_hbm, w_in.at[0], local_sem.at[1 + 2 * heads]),
        pltpu.make_async_copy(second_hbm, w_in.at[1], local_sem.at[2 + 2 * heads]),
    ]
    ids_copy = pltpu.make_async_copy(seg_hbm, seg_ref, local_sem.at[3 + 2 * heads])
    locals_ = [pltpu.make_async_copy(q_hbm.at[0, :, mine], qbuf.at[q_rows(x)], local_sem.at[0])]
    for h in range(heads):
        for i, source in enumerate((k_hbm, v_hbm)):
            locals_.append(
                pltpu.make_async_copy(
                    source.at[0, :, head_of(x, h)], kvbuf.at[h, i, token_rows(y, x)], local_sem.at[1 + 2 * h + i]
                )
            )
    for copy in weights + locals_ + [ids_copy]:
        copy.start()

    barrier = pltpu.get_barrier_semaphore()
    for partner in partners:
        pl.semaphore_signal(barrier, inc=1, device_id=partner, device_id_type=MESH)
    pl.semaphore_wait(barrier, len(partners))

    def copy_of(name, arriving):
        kind = name[0]
        if kind == "wy":
            j = name[1]
            sign = 1 if j > 0 else -1
            src = dst = wbuf.at[y_at(j if arriving else j - sign), z]
            who = to(fsdp=y_at(-sign) * 2 + x)
        elif kind == "wz":
            slot, k = name[1:]
            way = 1 if k > 0 else -1
            src = dst = wbuf.at[y_at(offsets[slot]), z_at(-k if arriving else -(k - way))]
            if abs(offsets[slot]) == 1 and LAST:
                src = dst = src.at[:, :split]
            who = to(dp=z_at(way))
        elif kind == "yl":
            j = name[1]
            src = dst = wbuf.at[y_at(j if arriving else 0), :, :, split:]
            who = to(fsdp=y_at(-j) * 2 + x)
        elif kind == "xq":
            dst = qbuf.at[q_rows(1 - x if arriving else x)]
            src = dst if arriving else q_hbm.at[0, :, theirs]
            who = to(fsdp=x_other)
        elif kind == "x":
            h, i = name[1:]
            dst = kvbuf.at[h, i, token_rows(y, 1 - x if arriving else x)]
            src = dst if arriving else (k_hbm, v_hbm)[i].at[0, :, head_of(1 - x, h)]
            who = to(fsdp=x_other)
        elif kind == "kv":
            h, own, k = name[1:]
            way = 1 if k > 0 else -1
            part_x = x if own else 1 - x
            src = dst = kvbuf.at[h, :, token_rows(y_at(-k if arriving else -(k - way)), part_x)]
            who = to(fsdp=y_at(way) * 2 + x)
        elif kind == "a":
            h, half = name[1:]
            src = dst = attbuf.at[((1 - x) if arriving else x) * heads + h, half * rows : (half + 1) * rows]
            who = to(fsdp=x_other)
        elif kind == "c":
            slot = name[1]
            dst = c_recv.at[slot]
            src = dst if arriving else p_all.at[slot, :, 1 - core]
            who = to(tensor=t_core)
        else:
            slot, r = name[1:]
            dst = e_recv.at[r, slot]
            src = dst if arriving else s_send.at[r, slot]
            who = partners[(2, 3, 0)[r]]
        i = ids[name]
        return pltpu.make_async_remote_copy(
            src_ref=src, dst_ref=dst, send_sem=send_sem.at[i], recv_sem=recv_sem.at[i],
            device_id=who, device_id_type=MESH,
        )

    def blend():
        for copy in weights:
            copy.wait()
        coef = blend_ref[0]
        mixed = (1.0 - coef) * w_in[0].astype(jnp.float32) + coef * w_in[1].astype(jnp.float32)
        wbuf[y, z] = mixed.astype(jnp.bfloat16)

    def mask():
        ids_copy.wait()
        count = 2 * rows
        row = seg_ref[:, pl.ds(pl.multiple_of(y * count, count), count)].astype(jnp.float32)
        on = lax.broadcasted_iota(jnp.int32, (count, count), 0) == lax.broadcasted_iota(jnp.int32, (count, count), 1)
        column = jnp.sum(jnp.where(on, jnp.broadcast_to(row, (count, count)), 0.0), axis=1, keepdims=True)
        keys = seg_ref[...].astype(jnp.float32)
        bias[...] = jnp.where(column == keys, jnp.float32(0.0), jnp.float32(-1e30))

    def scores_of(h, half, j):
        at, cols = slice(half * rows, (half + 1) * rows), slice(h * HEAD_DIM, (h + 1) * HEAD_DIM)
        keys = pl.ds(pl.multiple_of(y_at(j) * 2 * rows, 2 * rows), 2 * rows)
        scores = lax.dot_general(qbuf[at, cols], kvbuf[h, 0, keys], NT, preferred_element_type=jnp.float32)
        return scores * HEAD_DIM ** (-0.5) + bias[at, keys], keys

    def near(h, half):
        blocks = [scores_of(h, half, j) for j in range(1 - n_y // 2, n_y // 2)]
        top = jnp.max(functools.reduce(jnp.maximum, [scores for scores, _ in blocks]), axis=1, keepdims=True)
        expos = [jnp.exp(scores - top) for scores, _ in blocks]
        total = jnp.sum(functools.reduce(jnp.add, expos), axis=1, keepdims=True)
        result = jnp.zeros((rows, HEAD_DIM), jnp.float32)
        for expo, (_, keys) in zip(expos, blocks):
            result += jnp.dot(expo.astype(jnp.bfloat16), kvbuf[h, 1, keys], preferred_element_type=jnp.float32)
        stats[h, half, 0] = jnp.broadcast_to(top, (rows, HEAD_DIM))
        stats[h, half, 1] = jnp.broadcast_to(total, (rows, HEAD_DIM))
        stats[h, half, 2] = result

    def far(h, half):
        scores, keys = scores_of(h, half, n_y // 2)
        before = stats[h, half, 0][:, :1]
        top = jnp.maximum(before, jnp.max(scores, axis=1, keepdims=True))
        expo, shrink = jnp.exp(scores - top), jnp.exp(before - top)
        total = stats[h, half, 1][:, :1] * shrink + jnp.sum(expo, axis=1, keepdims=True)
        result = jnp.dot(expo.astype(jnp.bfloat16), kvbuf[h, 1, keys], preferred_element_type=jnp.float32)
        result = (stats[h, half, 2] * shrink + result) / total
        attbuf[x * heads + h, half * rows : (half + 1) * rows, :] = result.astype(jnp.bfloat16)

    def product(slot, spans):
        at = y_at(offsets[slot])
        weight = jnp.concatenate(
            [wbuf[at, :, :, a * HEAD_DIM : b * HEAD_DIM].reshape(n_z * piece, (b - a) * HEAD_DIM) for a, b in spans], axis=1
        )
        attended = jnp.concatenate([attbuf[i] for a, b in spans for i in range(a, b)], axis=1)
        return lax.dot_general(weight, attended, NT, preferred_element_type=jnp.float32)

    def pre(slot):
        acc[slot] = product(slot, [(0, heads - 1), (heads, 2 * heads - 1)])

    def proj(slot):
        part = acc[slot] + product(slot, [(heads - 1, heads), (2 * heads - 1, 2 * heads)])
        p_all[slot] = part.astype(jnp.bfloat16).reshape(p_all.shape[1:])

    def add(slot):
        for away in range(2):
            hi = (1 - x_hi) if away else x_hi
            both = (p_all[slot, hi, core].astype(jnp.float32) + c_recv[slot, hi].astype(jnp.float32)).astype(jnp.bfloat16)
            first, second = both[:, :rows], both[:, rows:]
            keep = jnp.where(x == 0, first, second)
            move = jnp.where(x == 0, second, first)
            if away:
                s_send[0, slot] = keep
                s_send[1, slot] = move
            else:
                s_keep[slot] = keep
                s_send[2, slot] = move

    def total(slot):
        at = y_at(offsets[slot])
        per = n_z // 4
        own = s_keep[slot].astype(jnp.float32) + e_recv[0, slot].astype(jnp.float32)
        other = e_recv[1, slot].astype(jnp.float32) + e_recv[2, slot].astype(jnp.float32)
        for i in range(per):
            part = slice(i * piece, (i + 1) * piece)
            out_t[i, at, x] = own[part].astype(jnp.bfloat16)
            out_t[i, at, 1 - x] = other[part].astype(jnp.bfloat16)

    def last():
        eye = lax.broadcasted_iota(jnp.int32, (rows, rows), 0) == lax.broadcasted_iota(jnp.int32, (rows, rows), 1)
        eye = jnp.where(eye, 1.0, 0.0).astype(jnp.bfloat16)
        flat = out_t[...].reshape(out_ref.shape[2], rows)
        out_ref[0] = lax.dot_general(eye, flat, NT, preferred_element_type=jnp.float32).astype(jnp.bfloat16)

    def local():
        for copy in locals_:
            copy.wait()

    work = {
        "blend": blend, "mask": mask, "near": near, "far": far, "pre": pre, "proj": proj, "add": add, "sum": total, "last": last, "local": local,
    }
    for verb, name in order:
        if verb == "start":
            copy_of(name, False).start()
        elif verb == "wait":
            copy_of(name, True).wait_recv()
        elif verb == "sent":
            copy_of(name, False).wait_send()
        else:
            work[name[0]](*name[1:])


def per_device(n_y, n_z, query, key_in, value, segment_ids, blend, w_first, w_second):
    rows, width = query.shape[1], query.shape[2]
    heads = width // HEAD_DIM // 2
    half = width // 2
    patches = segment_ids.shape[1]
    piece = w_first.shape[0]
    nodes, offsets = plan(n_y, n_z, heads)
    order = order_of(nodes)
    ids = {}
    for node in nodes:
        if node.link is not None:
            ids[node.name] = len(ids)
    bf16, f32 = jnp.bfloat16, jnp.float32
    group = n_z // 4 * piece
    any_, vmem = pl.BlockSpec(memory_space=pl.ANY), pl.BlockSpec(memory_space=pltpu.VMEM)
    out_cols = 2 * n_y * group
    return pl.pallas_call(
        functools.partial(kernel, n_y, n_z, order, ids, offsets),
        out_shape=jax.ShapeDtypeStruct((1, rows, out_cols), bf16),
        in_specs=[any_, any_, any_, any_, pl.BlockSpec(memory_space=pltpu.SMEM), any_, any_],
        out_specs=vmem,
        scratch_shapes=[
            pltpu.VMEM((1, patches), jnp.int32),
            pltpu.VMEM((2, piece, width), bf16),
            pltpu.VMEM((heads, 2, patches, HEAD_DIM), bf16),
            pltpu.VMEM((2 * rows, half), bf16),
            pltpu.VMEM((2 * rows, patches), f32),
            pltpu.VMEM((heads, 2, 3, rows, HEAD_DIM), f32),
            pltpu.VMEM((n_y, n_z, piece, width), bf16),
            pltpu.VMEM((2 * heads, 2 * rows, HEAD_DIM), bf16),
            pltpu.VMEM((n_y, n_z * piece, 2 * rows), f32),
            pltpu.VMEM((n_y, 2, 2, group, 2 * rows), bf16),
            pltpu.VMEM((n_y, 2, group, 2 * rows), bf16),
            pltpu.VMEM((3, n_y, group, rows), bf16),
            pltpu.VMEM((n_y, group, rows), bf16),
            pltpu.VMEM((3, n_y, group, rows), bf16),
            pltpu.VMEM((n_z // 4, n_y, 2, piece, rows), bf16),
            pltpu.SemaphoreType.DMA((4 + 2 * heads,)),
            pltpu.SemaphoreType.DMA((len(ids),)),
            pltpu.SemaphoreType.DMA((len(ids),)),
        ],
        compiler_params=pltpu.CompilerParams(
            collective_id=0, has_side_effects=True, vmem_limit_bytes=62 * 1024 * 1024
        ),
    )(query, key_in, value, segment_ids, blend, w_first, w_second)


def solution(mesh):
    in_specs = (
        P("dp", "fsdp", "tensor"),
        P("dp", "fsdp", "tensor"),
        P("dp", "fsdp", "tensor"),
        P("dp", None),
        P(),
        P(("dp", "fsdp"), "tensor"),
        P(("dp", "fsdp"), "tensor"),
    )
    out_specs = P("dp", "fsdp", "tensor")
    body = functools.partial(per_device, mesh.shape["fsdp"] // 2, mesh.shape["dp"])
    return jax.shard_map(body, mesh=mesh, in_specs=in_specs, out_specs=out_specs, check_vma=False)
```
